32 devices in a mesh: slab: 4 (over y, x), fsdp: 8 (over z, core).
Axes of the slice: x: 2, y: 2, z: 4, core: 2. Of those that a mesh axis runs over, the one named last changes fastest.
Arguments:
- volume: bfloat16 [128, 128, 128], P('slab'), may hold values from -6 to 6
- noise: bfloat16 [128, 128, 128], P('slab'), may hold values from -6 to 6
- cotangent: bfloat16 [128, 128, 128], P('slab'), may hold values from -1.5 to 1.5
- patch_corner: int32 [4, 32, 3], P('slab'), may hold values from 0 to 96, as said below
- patch_count: int32 [4, 8], P('slab'), may hold values from 0 to 4, as said below
- patch_level: int32 [4, 32], P('slab'), may hold values from 0 to 999
- embed: bfloat16 [512, 2048], replicated, may hold values from -0.25 to 0.25
- unembed: bfloat16 [2048, 512], replicated, may hold values from -0.125 to 0.125
- level_table: bfloat16 [1000, 2048], replicated, may hold values from -6 to 6
- pos_embed: bfloat16 [256, 2048], replicated, may hold values from -3 to 3
- w_qkv: bfloat16 [2048, 3072], P('fsdp'), may hold values from -0.125 to 0.125
- w_out: bfloat16 [1024, 2048], P('fsdp'), may hold values from -0.1875 to 0.1875
Outputs:
- score: float32 [128, 128, 128], P('slab', 'fsdp')
- grad_qk: float32 [2048, 2048], P('fsdp', 'slab')
- grad_v: float32 [2048, 1024], P('fsdp', 'slab')
- grad_out: float32 [1024, 2048], P('fsdp', 'slab')
The draws below stay inside these ranges and needn't reach their ends.
Inputs may be any that keep to these rules, and one draw needn't show every extreme that they name: patch_corner[s, j] holds multiples of 8; z lies in slab s (s * 32 <= z < (s + 1) * 32) and z + 32 <= 128; y and x are at most 64; entries of slots that are not live are of the same form; the smallest and largest values are reached. `patch_count`: each slab's counts add up to exactly 16; in every slab some device has 4 live slots.
All inputs are finite; a program needn't handle non-finite values.
Results may differ from the reference program's by a relative error of at most 0.024.
Values may be sent and summed in bfloat16 or wider, within the bound.
No kernel may reach another device: no remote copies, remote signals or barrier semaphores. Data moves between devices by JAX's collectives and lax.ppermute only.
A program may use at most 128 MiB of HBM per device.

```python
import jax
import jax.numpy as jnp
from jax import lax

D = 2048
HEADS = 8
HD = 128
NLEV = 1000
EDGE = 8
PXY = 8
PZT = 4
PPD = 2
SZ = 32
NXY = 128
SLABS = 4
MEMBERS = 8
NZ = 128
TOK = 256
VOX = 512
LISTLEN = 32


def draw_patch_count(key, part):
    keys = jax.random.split(key, SLABS)
    quarter = max(MEMBERS // 4, 1)

    def one_slab(slab_key):
        ranks = jax.random.permutation(slab_key, MEMBERS).astype(jnp.int32)
        counts = jnp.full((MEMBERS,), PPD, jnp.int32)
        counts = jnp.where(ranks < quarter, 2 * PPD, counts)
        counts = jnp.where((ranks >= quarter) & (ranks < 2 * quarter), 0, counts)
        counts = jnp.where((ranks >= 2 * quarter) & (ranks < 3 * quarter), PPD + 1, counts)
        counts = jnp.where((ranks >= 3 * quarter) & (ranks < 4 * quarter), PPD - 1, counts)
        return counts
    return jax.vmap(one_slab)(keys)


def draw_patch_corner(key, part):
    key_z, key_y, key_x = jax.random.split(jax.random.fold_in(key, 7), 3)
    slab_number = jnp.arange(SLABS, dtype=jnp.int32)[:, None]
    slot_number = jnp.arange(LISTLEN, dtype=jnp.int32)[None, :]
    options = jnp.where(slab_number == SLABS - 1, (SZ - EDGE * PZT) // EDGE + 1, SZ // EDGE)
    raw = jax.random.randint(key_z, (SLABS, LISTLEN), 0, 1 << 20, dtype=jnp.int32)
    depth = slab_number * SZ + raw % options * EDGE
    span = (NXY - EDGE * PXY) // EDGE + 1
    rows_y = jax.random.randint(key_y, (SLABS, LISTLEN), 0, span, dtype=jnp.int32) * EDGE
    rows_x = jax.random.randint(key_x, (SLABS, LISTLEN), 0, span, dtype=jnp.int32) * EDGE
    first = (slab_number == 0) & (slot_number == 0)
    last = (slab_number == SLABS - 1) & (slot_number == LISTLEN - 1)
    depth = jnp.where(first, 0, jnp.where(last, NZ - EDGE * PZT, depth))
    rows_y = jnp.where(first, 0, jnp.where(last, NXY - EDGE * PXY, rows_y))
    rows_x = jnp.where(first, 0, jnp.where(last, NXY - EDGE * PXY, rows_x))
    return jnp.stack([depth, rows_y, rows_x], axis=-1).astype(jnp.int32)


def place_ends(entries, rng, smallest, top_value):
    longest = entries.shape.index(max(entries.shape))
    spots = []
    for shift in (0, 1):
        where = [jax.random.randint(jax.random.fold_in(rng, axis), (), 0, length) for axis, length in enumerate(entries.shape)]
        where[longest] = (where[longest] + shift) % entries.shape[longest]
        spots.append(tuple(where))
    return entries.at[spots[0]].set(smallest).at[spots[1]].set(top_value)


def level_of(key, shape, shards, low, high):
    gain, own = 1.0, jax.random.fold_in(key, 6)
    for position, parts in shards:
        draws = jnp.exp(jax.random.uniform(jax.random.fold_in(own, position), (parts,), jnp.float32, low / len(shards), high / len(shards)))
        gain = gain * jnp.repeat(draws, shape[position] // parts).reshape([-1 if axis == position else 1 for axis in range(len(shape))])
    return gain


def scatter_about(own_key, shape, scale, reach, shards=(), held_as=jnp.bfloat16):
    factor_of = level_of(own_key, shape, shards, -0.22, 0.18) if shards else 1.0
    array = jax.random.normal(own_key, shape, jnp.float32) * scale * factor_of
    return jnp.minimum(jnp.maximum(array, -reach), reach).astype(held_as)


def setup_inputs(seed: int = 0) -> dict:
    arg_keys = jax.random.split(jax.random.key(seed), 13)
    volume = scatter_about(arg_keys[0], (NZ, NXY, NXY), 1.0, 6.0, ((0, 4),))
    noise = scatter_about(arg_keys[1], (NZ, NXY, NXY), 1.0, 6.0, ((0, 4),))
    cotangent = scatter_about(arg_keys[2], (NZ, NXY, NXY), 0.25, 1.5, ((0, 4),))
    patch_corner = draw_patch_corner(jax.random.fold_in(arg_keys[12], 71), 0)
    patch_count = draw_patch_count(jax.random.fold_in(arg_keys[12], 71), 0)
    patch_level = place_ends(jax.random.randint(arg_keys[5], (SLABS, LISTLEN), 0, NLEV), jax.random.fold_in(arg_keys[5], 1), 0, NLEV - 1).astype(jnp.int32)
    embed = scatter_about(arg_keys[6], (VOX, D), VOX ** -0.5, 0.25)
    unembed = scatter_about(arg_keys[7], (D, VOX), D ** -0.5, 0.125)
    level_table = scatter_about(arg_keys[8], (NLEV, D), 1.0, 6.0)
    pos_embed = scatter_about(arg_keys[9], (TOK, D), 0.5, 3.0)
    w_qkv = scatter_about(arg_keys[10], (D, 3 * HEADS * HD), D ** -0.5, 0.125, ((0, 8),))
    w_out = scatter_about(arg_keys[11], (HEADS * HD, D), (HEADS * HD) ** -0.5, 0.1875, ((0, 8),))
    return {"volume": volume, "noise": noise, "cotangent": cotangent, "patch_corner": patch_corner, "patch_count": patch_count, "patch_level": patch_level, "embed": embed, "unembed": unembed, "level_table": level_table, "pos_embed": pos_embed, "w_qkv": w_qkv, "w_out": w_out}


def layer_normal(hidden):
    centre = hidden - lax.optimization_barrier(jnp.mean(hidden, axis=-1, keepdims=True))
    inverse = lax.rsqrt(lax.optimization_barrier(jnp.mean(centre * centre, axis=-1, keepdims=True)) + 1e-05)
    return (centre * inverse, inverse)

def head_normal(values):
    inverse = lax.rsqrt(lax.optimization_barrier(jnp.mean(values * values, axis=-1, keepdims=True)) + 1e-06)
    return (values * inverse, inverse)

def contract(form, left, right):
    return jnp.einsum(form, left.astype(jnp.float32), right.astype(jnp.float32))

def pick_patches(counts, corners, levels, member):
    slots = corners.shape[0] // counts.shape[0]
    live = (jnp.arange(slots, dtype=jnp.int32)[None, :] < counts[:, None]).reshape(-1).astype(jnp.int32)
    before = jnp.cumsum(live, dtype=jnp.int32) - live
    wanted = member * PPD + jnp.arange(PPD, dtype=jnp.int32)
    chosen = ((before[None, :] == wanted[:, None]) & (live[None, :] == 1)).astype(jnp.int32)
    chosen_corner = lax.optimization_barrier(jnp.sum(chosen[:, :, None] * corners[None, :, :], axis=1, dtype=jnp.int32))
    chosen_level = lax.optimization_barrier(jnp.sum(chosen * levels[None, :], axis=1, dtype=jnp.int32))
    return (chosen_corner, chosen_level)

def noise_factors(chosen_level):
    sigma_level = 0.5 * jnp.exp(jnp.log(8.0) * chosen_level.astype(jnp.float32) / (NLEV - 1))
    return (sigma_level, lax.rsqrt(1.0 + sigma_level * sigma_level))

def to_tokens(block):
    shaped = block.reshape(PZT, EDGE, PXY, EDGE, PXY, EDGE).transpose(0, 2, 4, 1, 3, 5)
    return shaped.reshape(PZT * PXY * PXY, EDGE * EDGE * EDGE)

def from_tokens(token_rows):
    shaped = token_rows.reshape(PZT, PXY, PXY, EDGE, EDGE, EDGE).transpose(0, 3, 1, 4, 2, 5)
    return shaped.reshape(PZT * EDGE, PXY * EDGE, PXY * EDGE)

def cut_patches(clean, noisy, tangent, z_starts, chosen_corner, chosen_level):
    sigma_level, factor = noise_factors(chosen_level)
    extent = (PZT * EDGE, PXY * EDGE, PXY * EDGE)
    token_list = []
    tangent_list = []
    for number in range(PPD):
        starts = (z_starts[number], chosen_corner[number, 1], chosen_corner[number, 2])
        field = lax.dynamic_slice(clean, starts, extent).astype(jnp.float32)
        field = field + sigma_level[number] * lax.dynamic_slice(noisy, starts, extent).astype(jnp.float32)
        token_list.append(to_tokens(field * factor[number]).astype(jnp.bfloat16))
        tangent_list.append(to_tokens(lax.dynamic_slice(tangent, starts, extent)))
    return (jnp.stack(token_list), jnp.stack(tangent_list))

def place_scores(buffer, z_starts, chosen_corner, patch_scores):
    extent = (PZT * EDGE, PXY * EDGE, PXY * EDGE)
    for number in range(PPD):
        starts = (z_starts[number], chosen_corner[number, 1], chosen_corner[number, 2])
        block = lax.dynamic_slice(buffer, starts, extent) + from_tokens(patch_scores[number])
        buffer = lax.dynamic_update_slice(buffer, block, starts)
    return buffer

def compute(token_rows, chosen_level, tangent_rows, embed, unembed, level_table, pos_embed, w_qkv, w_out):
    count, tokens_p, voxels = token_rows.shape
    width = embed.shape[1]
    inner = w_out.shape[0]
    heads = inner // HD
    score_scale = 1.0 / HD ** 0.5
    onehot = (chosen_level[:, None] == jnp.arange(level_table.shape[0], dtype=jnp.int32)[None, :]).astype(jnp.bfloat16)
    level_rows = jnp.dot(onehot, level_table, preferred_element_type=jnp.float32)
    hidden0 = jnp.dot(token_rows.reshape(count * tokens_p, voxels), embed, preferred_element_type=jnp.float32)
    hidden0 = hidden0.reshape(count, tokens_p, width) + level_rows[:, None, :] + pos_embed.astype(jnp.float32)[None]
    normed_f, unused = layer_normal(hidden0)
    normed = normed_f.astype(jnp.bfloat16).reshape(count * tokens_p, width)
    projected = jnp.dot(normed, w_qkv, preferred_element_type=jnp.float32).reshape(count, tokens_p, 3, heads, HD)
    query_n, query_r = head_normal(projected[:, :, 0])
    key_n, key_r = head_normal(projected[:, :, 1])
    query_b = query_n.astype(jnp.bfloat16)
    key_b = key_n.astype(jnp.bfloat16)
    value_b = projected[:, :, 2].astype(jnp.bfloat16)
    logits = contract('pqhd,pkhd->phqk', query_b, key_b) * score_scale
    expo = jnp.exp(logits)
    attention_p = expo / lax.optimization_barrier(jnp.sum(expo, axis=-1, keepdims=True))
    attention_b = attention_p.astype(jnp.bfloat16)
    attended = contract('phqk,pkhd->pqhd', attention_b, value_b).astype(jnp.bfloat16).reshape(count * tokens_p, inner)
    hidden1 = hidden0 + jnp.dot(attended, w_out, preferred_element_type=jnp.float32).reshape(count, tokens_p, width)
    feat_f, feat_r = layer_normal(hidden1)
    features = feat_f.astype(jnp.bfloat16).reshape(count * tokens_p, width)
    patch_scores = jnp.dot(features, unembed, preferred_element_type=jnp.float32).reshape(count, tokens_p, voxels)
    d_feat = jnp.dot(tangent_rows.reshape(count * tokens_p, voxels), unembed.T, preferred_element_type=jnp.float32)
    d_feat = d_feat.reshape(count, tokens_p, width)
    d_hidden = feat_r * (d_feat - lax.optimization_barrier(jnp.mean(d_feat, axis=-1, keepdims=True)) - feat_f * lax.optimization_barrier(jnp.mean(d_feat * feat_f, axis=-1, keepdims=True)))
    d_hidden = d_hidden.astype(jnp.bfloat16).reshape(count * tokens_p, width)
    grad_out_term = jnp.dot(attended.T, d_hidden, preferred_element_type=jnp.float32)
    d_att = jnp.dot(d_hidden, w_out.T, preferred_element_type=jnp.float32).astype(jnp.bfloat16)
    d_att = d_att.reshape(count, tokens_p, heads, HD)
    d_probs = contract('pqhd,pkhd->phqk', d_att, value_b)
    d_value = contract('phqk,pqhd->pkhd', attention_b, d_att).astype(jnp.bfloat16)
    row_total = lax.optimization_barrier(jnp.sum(d_probs * attention_p, axis=-1, keepdims=True))
    d_logits = (attention_p * (d_probs - row_total) * score_scale).astype(jnp.bfloat16)
    d_query_n = contract('phqk,pkhd->pqhd', d_logits, key_b)
    d_key_n = contract('phqk,pqhd->pkhd', d_logits, query_b)
    d_query = (query_r * (d_query_n - query_n * lax.optimization_barrier(jnp.mean(d_query_n * query_n, axis=-1, keepdims=True)))).astype(jnp.bfloat16)
    d_key = (key_r * (d_key_n - key_n * lax.optimization_barrier(jnp.mean(d_key_n * key_n, axis=-1, keepdims=True)))).astype(jnp.bfloat16)
    rows = count * tokens_p
    d_both = jnp.concatenate([d_query.reshape(rows, inner), d_key.reshape(rows, inner)], axis=1)
    grad_qk_term = jnp.dot(normed.T, d_both, preferred_element_type=jnp.float32)
    grad_v_term = jnp.dot(normed.T, d_value.reshape(rows, inner), preferred_element_type=jnp.float32)
    return (patch_scores, grad_qk_term, grad_v_term, grad_out_term)

def rounded(values):
    return lax.optimization_barrier(values.astype(jnp.bfloat16)).astype(jnp.float32)

def reference(volume, noise, cotangent, patch_corner, patch_count, patch_level, embed, unembed, level_table, pos_embed, w_qkv, w_out):
    members = patch_count.shape[1]
    slabs = patch_count.shape[0]
    inner = w_out.shape[0]

    def device_step(totals, device):
        score_sum, qk_sum, value_sum, out_sum = totals
        slab_number = device // members
        member_number = device % members
        counts = lax.dynamic_index_in_dim(patch_count, slab_number, 0, keepdims=False)
        corners = lax.dynamic_index_in_dim(patch_corner, slab_number, 0, keepdims=False)
        levels = lax.dynamic_index_in_dim(patch_level, slab_number, 0, keepdims=False)
        chosen_corner, chosen_level = pick_patches(counts, corners, levels, member_number)
        token_rows, tangent_rows = cut_patches(volume, noise, cotangent, chosen_corner[:, 0], chosen_corner, chosen_level)
        patch_scores, qk_term, value_term, out_term = compute(token_rows, chosen_level, tangent_rows, embed, unembed, level_table, pos_embed, w_qkv, w_out)
        buffer = place_scores(jnp.zeros(volume.shape, jnp.float32), chosen_corner[:, 0], chosen_corner, patch_scores)
        return ((score_sum + rounded(buffer), qk_sum + rounded(qk_term), value_sum + rounded(value_term), out_sum + rounded(out_term)), None)
    initial = (jnp.zeros(volume.shape, jnp.float32), jnp.zeros((w_qkv.shape[0], 2 * inner), jnp.float32), jnp.zeros((w_qkv.shape[0], inner), jnp.float32), jnp.zeros(w_out.shape, jnp.float32))
    results, unused = lax.scan(device_step, initial, jnp.arange(slabs * members, dtype=jnp.int32))
    return (results[0], results[1], results[2], results[3])
```

```python
import functools

import jax
import jax.numpy as jnp
from jax import lax
from jax.experimental import pallas as pl
from jax.experimental.pallas import tpu as pltpu
from jax.sharding import PartitionSpec as P

HD = 128
NLEV = 1000
EDGE = 8
PXY = 8
PZT = 4
PPD = 2
HALO = 24
TOK = PZT * PXY * PXY
VOX = EDGE * EDGE * EDGE
KINDS = 3
LANES = 128

F32 = jnp.float32
BF16 = jnp.bfloat16
VMEM = pltpu.MemorySpace.VMEM
SMEM = pltpu.MemorySpace.SMEM
PARAMS = pltpu.CompilerParams(vmem_limit_bytes=48 * 1024 * 1024)


def swap(block, axis, pairs):
    return lax.ppermute(block, axis, pairs)


def across(block, axis, size, k):
    return lax.ppermute(block, axis, [(i, i ^ k) for i in range(size)])


def rows_dot(left, right):
    return lax.dot_general(left, right, (((1,), (0,)), ((), ())), preferred_element_type=F32)


def last_dot(left, right):
    return lax.dot_general(left, right, (((1,), (1,)), ((), ())), preferred_element_type=F32)


def first_dot(left, right):
    return lax.dot_general(left, right, (((0,), (0,)), ((), ())), preferred_element_type=F32)


def pick_patches(counts, corners, levels, first, number):
    slots = corners.shape[0] // counts.shape[0]
    live = (
        (jnp.arange(slots, dtype=jnp.int32)[None, :] < counts[:, None])
        .reshape(-1)
        .astype(jnp.int32)
    )
    before = jnp.cumsum(live, dtype=jnp.int32) - live
    wanted = first + jnp.arange(number, dtype=jnp.int32)
    chosen = ((before[None, :] == wanted[:, None]) & (live[None, :] == 1)).astype(jnp.int32)
    chosen_corner = jnp.sum(chosen[:, :, None] * corners[None, :, :], axis=1, dtype=jnp.int32)
    chosen_level = jnp.sum(chosen * levels[None, :], axis=1, dtype=jnp.int32)
    return (chosen_corner, chosen_level)


def noise_factors(chosen_level):
    sigma_level = 0.5 * jnp.exp(jnp.log(8.0) * chosen_level.astype(F32) / (NLEV - 1))
    return (sigma_level, lax.rsqrt(1.0 + sigma_level * sigma_level))


def exchange_groups(tiles, lane):
    for bit in range(3):
        step = 1 << bit
        upper = ((lane >> (3 + bit)) & 1) == 1
        fresh = []
        for i in range(8):
            other = tiles[i ^ step]
            if i & step:
                moved = pltpu.roll(other, LANES - 8 * step, 1)
                fresh.append(jnp.where(upper, tiles[i], moved))
            else:
                moved = pltpu.roll(other, 8 * step, 1)
                fresh.append(jnp.where(upper, moved, tiles[i]))
        tiles = fresh
    return tiles


def cut_kernel(noisy, corner_ref, factor_ref, *refs):
    if noisy:
        field_ref, noise_ref, out_ref, work = refs
    else:
        field_ref, out_ref, work = refs
    number = pl.program_id(0)
    z0 = corner_ref[number, 0]
    y0 = corner_ref[number, 1]
    x0 = corner_ref[number, 2]
    lane = lax.broadcasted_iota(jnp.int32, (8, LANES), 1)
    low = lax.broadcasted_iota(jnp.int32, (64, LANES), 1) < 64
    for pair in range(PZT // 2):
        for ez in range(0, EDGE, 2):
            halves = []
            for half in range(2):
                z = z0 + (2 * pair + half) * EDGE + ez
                planes = []
                for odd in range(2):
                    plane = field_ref[z + odd, pl.ds(y0, PXY)].astype(F32)
                    if noisy:
                        noise = noise_ref[z + odd, pl.ds(y0, PXY)].astype(F32)
                        plane = (plane + factor_ref[number, 0] * noise) * factor_ref[number, 1]
                    plane = plane.reshape(64, LANES)
                    shift = lax.rem(LANES + 64 * odd - x0, LANES)
                    planes.append(pltpu.roll(plane, shift, 1))
                work[half] = jnp.where(low, planes[0], planes[1])
                tiles = [work[half, pl.ds(ey, 8, stride=8), :] for ey in range(8)]
                halves.append(exchange_groups(tiles, lane))
            for px in range(PXY):
                row = px * 32 + pair * 16
                both = jnp.concatenate([halves[0][px], halves[1][px]], axis=0)
                out_ref[0, row : row + 16, (ez // 2) * LANES : (ez // 2 + 1) * LANES] = both.astype(
                    BF16
                )


def cut_tokens(corner, factors, fields):
    count = corner.shape[0]
    shaped = [f.reshape(f.shape[0], f.shape[1] // 8, 8, LANES) for f in fields]
    whole = [pl.BlockSpec(f.shape, lambda i: (0, 0, 0, 0)) for f in shaped]
    return pl.pallas_call(
        functools.partial(cut_kernel, len(fields) == 2),
        grid=(count,),
        in_specs=[pl.BlockSpec(memory_space=SMEM)] * 2 + whole,
        out_specs=pl.BlockSpec((1, TOK, VOX), lambda i: (i, 0, 0)),
        out_shape=jax.ShapeDtypeStruct((count, TOK, VOX), BF16),
        scratch_shapes=[pltpu.VMEM((2, 64, LANES), F32)],
        compiler_params=PARAMS,
        name="cut_tokens",
    )(corner, factors, *shaped)


def place_kernel(corner_ref, *refs):
    score_refs = refs[:PPD]
    out_ref, buffer, work = refs[PPD:]
    lane = lax.broadcasted_iota(jnp.int32, (8, LANES), 1)
    wide = lax.broadcasted_iota(jnp.int32, (64, LANES), 1)
    buffer[...] = jnp.zeros_like(buffer)
    for number in range(PPD):
        z0 = corner_ref[number, 0]
        y0 = corner_ref[number, 1]
        x0 = corner_ref[number, 2]
        inside = (wide >= x0) & (wide < x0 + 64)
        for pz in range(PZT):
            for ez in range(0, EDGE, 2):
                tiles = [
                    score_refs[number][
                        px * 32 + pz * 8 : px * 32 + pz * 8 + 8,
                        (ez // 2) * LANES : (ez // 2 + 1) * LANES,
                    ].astype(F32)
                    for px in range(PXY)
                ]
                tiles = exchange_groups(tiles, lane)
                slot = (ez // 2) % 2
                for ey in range(8):
                    work[slot, pl.ds(ey, 8, stride=8), :] = tiles[ey]
                both = work[slot]
                for odd in range(2):
                    plane = pltpu.roll(both, lax.rem(LANES + x0 - 64 * odd, LANES), 1)
                    plane = jnp.where(inside, plane, 0.0).reshape(PXY, 8, LANES)
                    z = z0 + pz * EDGE + ez + odd
                    buffer[z, pl.ds(y0, PXY)] += plane
    out_ref[...] = buffer[...].astype(BF16)


def place_scores(corner, scores, planes, rows):
    shape = (planes, rows // 8, 8, LANES)
    out = pl.pallas_call(
        place_kernel,
        in_specs=[pl.BlockSpec(memory_space=SMEM)] + [pl.BlockSpec(memory_space=VMEM)] * PPD,
        out_specs=pl.BlockSpec(memory_space=VMEM),
        out_shape=jax.ShapeDtypeStruct(shape, BF16),
        scratch_shapes=[pltpu.VMEM(shape, F32), pltpu.VMEM((2, 64, LANES), F32)],
        compiler_params=PARAMS,
        name="place_scores",
    )(corner, *scores)
    return out.reshape(planes, rows, LANES)


def fold_kernel(members, me_ref, embed_ref, pos_ref, level_ref, *refs):
    w_refs, out_ref = refs[:members], refs[members]
    me = me_ref[0]
    width = embed_ref.shape[1]
    depth = w_refs[0].shape[0]
    start = 0
    column = jnp.zeros((1, HD), F32)
    for k in range(members):
        column += jnp.sum(w_refs[k][...].astype(F32), axis=0, keepdims=True)
    for part in (embed_ref, pos_ref, level_ref):
        rows = part.shape[0]
        total = jnp.zeros((rows, HD), F32)
        for k in range(members):
            at = pl.multiple_of(jnp.bitwise_xor(me, k) * depth, LANES)
            total += rows_dot(part[:, pl.ds(at, depth)], w_refs[k][...])
        mean = jnp.sum(part[...].astype(F32), axis=1, keepdims=True) / width
        out_ref[start : start + rows, :] = (total - mean * column).astype(BF16)
        start += rows


def fold_weights(me, embed, pos, level, blocks):
    rows = embed.shape[0] + pos.shape[0] + level.shape[0]
    return pl.pallas_call(
        functools.partial(fold_kernel, len(blocks)),
        in_specs=[pl.BlockSpec(memory_space=SMEM)]
        + [pl.BlockSpec(memory_space=VMEM)] * (3 + len(blocks)),
        out_specs=pl.BlockSpec(memory_space=VMEM),
        out_shape=jax.ShapeDtypeStruct((rows, HD), BF16),
        compiler_params=PARAMS,
        name="fold_weights",
    )(me, embed, pos, level, *blocks)


def head_normal(values):
    inverse = lax.rsqrt(jnp.mean(values * values, axis=-1, keepdims=True) + 1e-06)
    return (values * inverse, inverse)


def attention(info_ref, token_ref, scale_ref, fold_refs):
    tokens = token_ref[0]
    rows = fold_refs[0].shape[1]
    patches = rows - VOX - TOK
    where_level = info_ref[1] + jnp.bitwise_xor(info_ref[0], pl.program_id(0)) * PPD
    onehot = (lax.broadcasted_iota(jnp.int32, (TOK, patches), 1) == where_level).astype(BF16)
    scale = jnp.transpose(jnp.broadcast_to(scale_ref[0], (HD, TOK)))
    kinds = []
    for ref in fold_refs:
        total = rows_dot(tokens, ref[0, :VOX])
        total += ref[0, VOX : VOX + TOK].astype(F32)
        total += rows_dot(onehot, ref[0, VOX + TOK :])
        kinds.append(total * scale)
    query_n, query_r = head_normal(kinds[0])
    key_n, key_r = head_normal(kinds[1])
    query_b, key_b, value_b = (query_n.astype(BF16), key_n.astype(BF16), kinds[2].astype(BF16))
    expo = jnp.exp(last_dot(query_b, key_b) * (1.0 / HD**0.5))
    probs = expo / jnp.sum(expo, axis=-1, keepdims=True)
    return (
        tokens,
        onehot,
        scale,
        (query_n, query_r, query_b),
        (key_n, key_r, key_b),
        value_b,
        probs,
        probs.astype(BF16),
    )


def forward_kernel(info_ref, token_ref, scale_ref, q_ref, k_ref, v_ref, out_ref):
    state = attention(info_ref, token_ref, scale_ref, (q_ref, k_ref, v_ref))
    out_ref[0] = rows_dot(state[7], state[5]).astype(BF16)


def backward_kernel(info_ref, token_ref, scale_ref, q_ref, k_ref, v_ref, d_ref, last_ref, out_ref):
    step = pl.program_id(0)
    tokens, onehot, scale, query, key, value_b, probs, probs_b = attention(
        info_ref, token_ref, scale_ref, (q_ref, k_ref, v_ref)
    )
    query_n, query_r, query_b = query
    key_n, key_r, key_b = key
    d_att = d_ref[0]
    d_probs = last_dot(d_att, value_b)
    d_value = first_dot(probs_b, d_att)
    row_total = jnp.sum(d_probs * probs, axis=-1, keepdims=True)
    d_logits = (probs * (d_probs - row_total) * (1.0 / HD**0.5)).astype(BF16)
    d_query_n = rows_dot(d_logits, key_b)
    d_key_n = first_dot(d_logits, query_b)
    d_query = query_r * (
        d_query_n - query_n * jnp.mean(d_query_n * query_n, axis=-1, keepdims=True)
    )
    d_key = key_r * (d_key_n - key_n * jnp.mean(d_key_n * key_n, axis=-1, keepdims=True))

    @pl.when(step == 0)
    def _():
        out_ref[...] = last_ref[...]

    for kind, grad in enumerate((d_query, d_key, d_value)):
        grad = (grad * scale).astype(BF16)
        out_ref[kind, :VOX] += first_dot(tokens, grad)
        out_ref[kind, VOX : VOX + TOK] += grad.astype(F32)
        out_ref[kind, VOX + TOK :] += first_dot(onehot, grad)


def attention_specs(number, heads, rows):
    def at_patch(k, info):
        return (jnp.bitwise_xor(info[0], k) * PPD + number, 0, 0)

    def kind_spec(kind):
        return pl.BlockSpec((1, rows, HD), lambda k, info: (info[2 + kind], 0, 0))

    return [
        pl.BlockSpec((1, TOK, VOX), at_patch),
        pl.BlockSpec((1, 1, TOK), lambda k, info: (k, 0, 0)),
    ] + [kind_spec(kind) for kind in range(KINDS)]


def forward_heads(number, info, tokens, scale, folds):
    heads = scale.shape[0]
    rows = folds.shape[1]
    return pl.pallas_call(
        forward_kernel,
        grid_spec=pltpu.PrefetchScalarGridSpec(
            num_scalar_prefetch=1,
            grid=(heads,),
            in_specs=attention_specs(number, heads, rows),
            out_specs=pl.BlockSpec((1, TOK, HD), lambda k, info: (k, 0, 0)),
        ),
        out_shape=jax.ShapeDtypeStruct((heads, TOK, HD), BF16),
        compiler_params=PARAMS,
        name="forward_heads",
    )(info, tokens, scale, folds, folds, folds)


def backward_heads(number, info, tokens, scale, folds, d_att, last):
    heads = scale.shape[0]
    rows = folds.shape[1]
    whole = pl.BlockSpec((KINDS, rows, HD), lambda k, info: (0, 0, 0))
    return pl.pallas_call(
        backward_kernel,
        grid_spec=pltpu.PrefetchScalarGridSpec(
            num_scalar_prefetch=1,
            grid=(heads,),
            in_specs=attention_specs(number, heads, rows)
            + [pl.BlockSpec((1, TOK, HD), lambda k, info: (k, 0, 0)), whole],
            out_specs=whole,
        ),
        out_shape=jax.ShapeDtypeStruct((KINDS, rows, HD), F32),
        compiler_params=PARAMS,
        name="backward_heads",
    )(info, tokens, scale, folds, folds, folds, d_att, last)


def output_kernel(heads, me_ref, hidden_ref, cot_ref, w_ref, unembed_ref, *refs):
    att_refs = refs[:heads]
    score_ref, wide_ref, d_hidden_ref, d_att_ref, work = refs[heads:]
    me = me_ref[0]
    for k in range(heads):
        at = pl.multiple_of(jnp.bitwise_xor(me, k) * HD, HD)
        wide_ref[:, pl.ds(at, HD)] = att_refs[k][...]
    hidden = hidden_ref[...] + rows_dot(wide_ref[...], w_ref[...])
    centre = hidden - jnp.mean(hidden, axis=-1, keepdims=True)
    inverse = lax.rsqrt(jnp.mean(centre * centre, axis=-1, keepdims=True) + 1e-05)
    feat = centre * inverse
    score_ref[...] = rows_dot(feat.astype(BF16), unembed_ref[...])
    d_feat = last_dot(cot_ref[...], unembed_ref[...])
    d_hidden = inverse * (
        d_feat
        - jnp.mean(d_feat, axis=-1, keepdims=True)
        - feat * jnp.mean(d_feat * feat, axis=-1, keepdims=True)
    )
    d_hidden = d_hidden.astype(BF16)
    d_hidden_ref[...] = d_hidden
    work[...] = last_dot(d_hidden, w_ref[...]).astype(BF16)
    for k in range(heads):
        at = pl.multiple_of(jnp.bitwise_xor(me, k) * HD, HD)
        d_att_ref[k] = work[:, pl.ds(at, HD)]


def output_part(me, hidden, cot, w_out, unembed, attended):
    heads = len(attended)
    inner, width = w_out.shape
    shape = jax.ShapeDtypeStruct
    return pl.pallas_call(
        functools.partial(output_kernel, heads),
        in_specs=[pl.BlockSpec(memory_space=SMEM)]
        + [pl.BlockSpec(memory_space=VMEM)] * (4 + heads),
        out_specs=[pl.BlockSpec(memory_space=VMEM)] * 4,
        out_shape=[
            shape((TOK, VOX), F32),
            shape((TOK, inner), BF16),
            shape((TOK, width), BF16),
            shape((heads, TOK, HD), BF16),
        ],
        scratch_shapes=[pltpu.VMEM((TOK, inner), BF16)],
        compiler_params=PARAMS,
        name="output_part",
    )(me, hidden, cot, w_out, unembed, *attended)


def expand_kernel(heads, blocks, me_ref, embed_ref, pos_ref, level_ref, own_ref, *refs):
    in_refs, (out_ref, work) = refs[:-2], refs[-2:]
    total = own_ref[...].astype(F32)
    for ref in in_refs:
        total += ref[...].astype(F32)
    total = total.astype(BF16)
    split = embed_ref.shape[0]
    after = split + pos_ref.shape[0]
    grad = first_dot(embed_ref[...], total[:split])
    grad += first_dot(pos_ref[...], total[split:after])
    grad += first_dot(level_ref[...], total[after:])
    grad -= jnp.mean(grad, axis=0, keepdims=True)
    work[...] = grad.astype(BF16)
    depth = out_ref.shape[1]
    base = (me_ref[0] // heads) * heads
    for k in range(heads):
        member = base + jnp.bitwise_xor(lax.rem(me_ref[0], heads), k)
        out_ref[k] = work[pl.ds(pl.multiple_of(member * depth, depth), depth), :]


def expand_sums(me, heads, depth, embed, pos, level, own, others):
    width = embed.shape[1]
    columns = own.shape[1]
    return pl.pallas_call(
        functools.partial(expand_kernel, heads, len(others)),
        in_specs=[pl.BlockSpec(memory_space=SMEM)]
        + [pl.BlockSpec(memory_space=VMEM)] * (4 + len(others)),
        out_specs=pl.BlockSpec(memory_space=VMEM),
        out_shape=jax.ShapeDtypeStruct((heads, depth, columns), BF16),
        scratch_shapes=[pltpu.VMEM((width, columns), BF16)],
        compiler_params=PARAMS,
        name="expand_sums",
    )(me, embed, pos, level, own, *others)


def on_device(
    slabs,
    members,
    volume,
    noise,
    cotangent,
    patch_corner,
    patch_count,
    patch_level,
    embed,
    unembed,
    level_table,
    pos_embed,
    w_qkv,
    w_out,
):
    planes, side = volume.shape[:2]
    width = embed.shape[1]
    inner = w_out.shape[0] * members
    heads = inner // HD
    groups = members // heads
    depth = w_qkv.shape[0]
    slab = lax.axis_index("slab")
    member = lax.axis_index("fsdp")
    group, head = member // heads, member % heads
    core = member % 2

    def in_group(block, k):
        pairs = [(i, (i // heads) * heads + ((i % heads) ^ k)) for i in range(members)]
        return swap(block, "fsdp", pairs)

    def among_slabs(block, k):
        return across(block, "slab", slabs, k)

    me = jnp.reshape(member, (1,)).astype(jnp.int32)

    kind = slab % KINDS
    w_blocks = []
    for k in range(members):
        to = (member ^ k) % heads
        block = lax.dynamic_slice(w_qkv, (0, kind * inner + to * HD), (depth, HD))
        w_blocks.append(across(block, "fsdp", members, k) if k else block)

    part = HALO // 2
    rims = jnp.stack(
        [
            lax.dynamic_slice(f, (core * part, 0, 0), (part, side, side))
            for f in (volume, noise, cotangent)
        ]
    )
    rims = swap(rims, "slab", [(i, i - 1) for i in range(1, slabs)])
    other = across(rims, "fsdp", members, 1)
    first = jnp.where(core == 0, rims, other)
    second = jnp.where(core == 0, other, rims)
    clean, noisy, tangent = [
        jnp.concatenate([f, first[i], second[i]], axis=0)
        for i, f in enumerate((volume, noise, cotangent))
    ]

    total = members * PPD
    all_corner, all_level = pick_patches(
        patch_count[0], patch_corner[0], patch_level[0], 0, total
    )
    group_first = group * heads * PPD
    corner = lax.dynamic_slice(all_corner, (group_first, 0), (heads * PPD, 3))
    level = lax.dynamic_slice(all_level, (group_first,), (heads * PPD,))
    corner = jnp.stack([corner[:, 0] - slab * planes, corner[:, 1] // 8, corner[:, 2]], axis=1)
    own_corner = lax.dynamic_slice(corner, (head * PPD, 0), (PPD, 3))
    levels = jnp.stack(
        [among_slabs(all_level, k) if k else all_level for k in range(slabs)]
    )
    levels = jnp.take(levels, jnp.arange(slabs, dtype=jnp.int32) ^ slab, axis=0).reshape(-1)
    onehot = (levels[:, None] == jnp.arange(level_table.shape[0], dtype=jnp.int32)[None, :]).astype(
        BF16
    )
    level_rows = jnp.dot(onehot, level_table, preferred_element_type=F32).astype(BF16)

    pos = pos_embed.reshape(PZT * PXY, PXY, width).transpose(1, 0, 2).reshape(TOK, width)

    sigma_level, factor = noise_factors(level)
    tokens = cut_tokens(corner, jnp.stack([sigma_level, factor], axis=1), (clean, noisy))
    tangents = cut_tokens(own_corner, jnp.zeros((PPD, 2), F32), (tangent,))

    own_tokens = lax.dynamic_slice(tokens, (head * PPD, 0, 0), (PPD, TOK, VOX))
    own_place = slab * total + member * PPD
    own_rows = lax.dynamic_slice(level_rows, (own_place, 0), (PPD, width)).astype(F32)
    hidden = jnp.dot(own_tokens.reshape(PPD * TOK, VOX), embed, preferred_element_type=F32)
    hidden = hidden.reshape(PPD, TOK, width) + own_rows[:, None, :] + pos.astype(F32)[None]
    centre = hidden - jnp.mean(hidden, axis=-1, keepdims=True)
    scale = lax.rsqrt(jnp.mean(centre * centre, axis=-1) + 1e-05)[None]
    step = 1
    while step < heads:
        scale = jnp.concatenate([scale, in_group(scale, step)], axis=0)
        step *= 2
    scales = [scale[:, n].reshape(heads, 1, TOK) for n in range(PPD)]

    fold = fold_weights(me, embed, pos, level_rows, w_blocks)
    folds = jnp.stack([among_slabs(fold, k) if k else fold for k in range(slabs)])
    full_out = lax.all_gather(w_out, "fsdp", axis=0, tiled=True)

    infos = [
        jnp.stack([head, slab * total + group_first + n] + [slab ^ j for j in range(KINDS)]).astype(
            jnp.int32
        )
        for n in range(PPD)
    ]
    head_me = jnp.reshape(head, (1,)).astype(jnp.int32)
    scores, wides, d_hiddens, d_atts = [], [], [], []
    for n in range(PPD):
        att = forward_heads(n, infos[n], tokens, scales[n], folds)
        attended = [in_group(att[k], k) if k else att[0] for k in range(heads)]
        score, wide, d_hidden, d_att = output_part(
            head_me, hidden[n], tangents[n], full_out, unembed, attended
        )
        scores.append(score)
        wides.append(wide)
        d_hiddens.append(d_hidden)
        d_atts.append(jnp.stack([in_group(d_att[k], k) if k else d_att[0] for k in range(heads)]))
    rows = fold.shape[0]
    sums = jnp.zeros((KINDS, rows, HD), F32)
    for n in range(PPD):
        sums = backward_heads(n, infos[n], tokens, scales[n], folds, d_atts[n], sums)
    sums = sums.astype(BF16)

    half = slabs // 2

    def sums_for(target):
        qk = lax.dynamic_index_in_dim(sums, target // half, 0, keepdims=False)
        return jnp.concatenate([qk, sums[2]], axis=1)

    others = [among_slabs(sums_for(slab ^ k), k) for k in range(1, slabs)]
    own = sums_for(slab)
    if groups > 1:
        gathered = own.astype(F32)
        for block in others:
            gathered += block.astype(F32)
        own = gathered.astype(BF16)
        others = [
            swap(own, "fsdp", [(i, ((i // heads) ^ g) * heads + i % heads) for i in range(members)])
            for g in range(1, groups)
        ]
    blocks = expand_sums(me, heads, depth, embed, pos, level_rows, own, others)
    qk_heads = heads // half
    v_heads = heads // slabs
    pairs_of = []
    for k in range(heads):
        pairs = []
        for s in range(slabs):
            for i in range(members):
                h = i % heads
                if h // qk_heads == s % half or h // v_heads == s:
                    j = (i // heads) * heads + (h ^ k)
                    pairs.append((s * members + i, s * members + j))
        pairs_of.append(pairs)
    arrived = jnp.stack(
        [swap(blocks[k], ("slab", "fsdp"), pairs_of[k]) if k else blocks[0] for k in range(heads)]
    )

    def from_heads(first, number, column):
        pieces = [
            lax.dynamic_index_in_dim(arrived, head ^ (first + i), 0, keepdims=False)[
                :, column * HD : (column + 1) * HD
            ]
            for i in range(number)
        ]
        return jnp.concatenate(pieces, axis=1).astype(F32)

    grad_qk = from_heads((slab % half) * qk_heads, qk_heads, 0)
    grad_v = from_heads(slab * v_heads, v_heads, 1)

    out_term = first_dot(
        jnp.concatenate(wides, axis=0), jnp.concatenate(d_hiddens, axis=0)
    ).astype(BF16)
    out_part = lax.psum_scatter(out_term, "fsdp", scatter_dimension=0, tiled=True)
    grad_out = lax.psum_scatter(out_part, "slab", scatter_dimension=1, tiled=True).astype(F32)

    buffer = place_scores(own_corner, scores, planes + HALO, side)
    summed = lax.psum_scatter(buffer, "fsdp", scatter_dimension=1, tiled=True)
    arrived_rim = swap(summed[planes:], "slab", [(i, i + 1) for i in range(slabs - 1)])
    score = summed[:planes].astype(F32).at[:HALO].add(arrived_rim.astype(F32))
    return (score, grad_qk, grad_v, grad_out)


def solution(mesh):
    placed = (
        P("slab", None, None),
        P("slab", None, None),
        P("slab", None, None),
        P("slab", None, None),
        P("slab", None),
        P("slab", None),
        P(),
        P(),
        P(),
        P(),
        P("fsdp", None),
        P("fsdp", None),
    )
    return jax.shard_map(
        functools.partial(on_device, mesh.shape["slab"], mesh.shape["fsdp"]),
        mesh=mesh,
        in_specs=placed,
        out_specs=(
            P("slab", "fsdp", None),
            P("fsdp", "slab"),
            P("fsdp", "slab"),
            P("fsdp", "slab"),
        ),
        check_vma=False,
    )
```

```python
import functools

import jax
import jax.numpy as jnp
from jax import lax
from jax.experimental import pallas as pl
from jax.experimental.pallas import tpu as pltpu
from jax.sharding import PartitionSpec as P

HD = 128
NLEV = 1000
EDGE = 8
PXY = 8
PZT = 4
PPD = 2
HALO = 24
TOK = PZT * PXY * PXY
VOX = EDGE * EDGE * EDGE
KINDS = 3
LANES = 128

F32 = jnp.float32
BF16 = jnp.bfloat16
VMEM = pltpu.MemorySpace.VMEM
SMEM = pltpu.MemorySpace.SMEM
HBM = pltpu.MemorySpace.HBM
PARAMS = pltpu.CompilerParams(vmem_limit_bytes=20 * 1024 * 1024)


def cost(microseconds):
    return pl.CostEstimate(
        flops=int(microseconds * 1e9), bytes_accessed=1 << 20, transcendentals=0
    )


def swap(block, axis, pairs):
    return lax.ppermute(block, axis, pairs)


def after(value, *others):
    return lax.optimization_barrier((value, others))[0]


def across(block, axis, size, k):
    return lax.ppermute(block, axis, [(i, i ^ k) for i in range(size)])


def rows_dot(left, right):
    return lax.dot_general(left, right, (((1,), (0,)), ((), ())), preferred_element_type=F32)


def last_dot(left, right):
    return lax.dot_general(left, right, (((1,), (1,)), ((), ())), preferred_element_type=F32)


def first_dot(left, right):
    return lax.dot_general(left, right, (((0,), (0,)), ((), ())), preferred_element_type=F32)


def pick_patches(counts, corners, levels, first, number):
    slots = corners.shape[0] // counts.shape[0]
    live = (
        (jnp.arange(slots, dtype=jnp.int32)[None, :] < counts[:, None])
        .reshape(-1)
        .astype(jnp.int32)
    )
    before = jnp.cumsum(live, dtype=jnp.int32) - live
    wanted = first + jnp.arange(number, dtype=jnp.int32)
    chosen = ((before[None, :] == wanted[:, None]) & (live[None, :] == 1)).astype(jnp.int32)
    chosen_corner = jnp.sum(chosen[:, :, None] * corners[None, :, :], axis=1, dtype=jnp.int32)
    chosen_level = jnp.sum(chosen * levels[None, :], axis=1, dtype=jnp.int32)
    return (chosen_corner, chosen_level)


def noise_factors(chosen_level):
    sigma_level = 0.5 * jnp.exp(jnp.log(8.0) * chosen_level.astype(F32) / (NLEV - 1))
    return (sigma_level, lax.rsqrt(1.0 + sigma_level * sigma_level))


def exchange_groups(tiles, lane):
    for bit in range(3):
        step = 1 << bit
        upper = ((lane >> (3 + bit)) & 1) == 1
        fresh = []
        for i in range(8):
            other = tiles[i ^ step]
            if i & step:
                moved = pltpu.roll(other, LANES - 8 * step, 1)
                fresh.append(jnp.where(upper, tiles[i], moved))
            else:
                moved = pltpu.roll(other, 8 * step, 1)
                fresh.append(jnp.where(upper, moved, tiles[i]))
        tiles = fresh
    return tiles


def lane_order():
    row = lax.broadcasted_iota(jnp.int32, (8 * LANES, 8 * LANES), 0)
    lane = lax.broadcasted_iota(jnp.int32, (8 * LANES, 8 * LANES), 1)
    source = (lane // 8) % 8 * LANES + (lane // 64) % 2 * 64 + lane // LANES * 8 + lane % 8
    return (row == source).astype(BF16)


def cut_patches(count, corner_ref, factor_ref, order_ref, fields, pairs, work, wide, out_ref):
    row = lax.broadcasted_iota(jnp.int32, (2 * LANES, LANES), 0)
    lane = lax.broadcasted_iota(jnp.int32, (2 * LANES, LANES), 1)
    source = lane // 64 * LANES + lane % 64

    def body(number, carry):
        z0 = corner_ref[number, 0]
        y0 = corner_ref[number, 1]
        for pz in range(PZT):
            for ez in range(EDGE):
                z = z0 + pz * EDGE + ez
                plane = fields[0][z, pl.ds(y0, PXY)].astype(F32)
                if len(fields) == 2:
                    noise = fields[1][z, pl.ds(y0, PXY)].astype(F32)
                    plane = (plane + factor_ref[number, 0] * noise) * factor_ref[number, 1]
                at = (pz * 4 + ez // 2) * 64
                half = ez % 2 * LANES
                pairs[at : at + 64, half : half + LANES] = plane.reshape(64, LANES).astype(BF16)
        select = (row == source + corner_ref[number, 2]).astype(BF16)
        work[...] = rows_dot(pairs[...], select)
        at = pl.multiple_of(number * LANES, LANES)
        for ey in range(EDGE):
            tile = work[pl.ds(ey, LANES, stride=8), :]
            wide[pl.ds(at, LANES), ey * LANES : (ey + 1) * LANES] = tile.astype(BF16)
        return carry

    lax.fori_loop(0, count, body, 0)
    for two in range(PXY // 2):
        moved = rows_dot(wide[...], order_ref[:, two * 2 * LANES : (two + 1) * 2 * LANES])
        for number in range(count):
            for pair in range(PZT // 2):
                for ez in range(EDGE // 2):
                    first = number * LANES + (2 * pair * 4 + ez) * 8
                    second = first + 4 * 8
                    both = jnp.concatenate(
                        [moved[first : first + 8], moved[second : second + 8]], axis=0
                    ).astype(BF16)
                    for px in range(2):
                        at = (two * 2 + px) * 32 + pair * 16
                        out_ref[number, at : at + 16, ez * LANES : (ez + 1) * LANES] = both[
                            :, px * LANES : (px + 1) * LANES
                        ]


def cut_scratch(count):
    return [
        pltpu.VMEM((16 * 64, 2 * LANES), BF16),
        pltpu.VMEM((16 * 64, LANES), F32),
        pltpu.VMEM((count * LANES, 8 * LANES), BF16),
    ]


def join_kernel(count, number, core_ref, corner_ref, factor_ref, order_ref, *refs):
    field_refs, (mine_ref, other_ref) = refs[:number], refs[number : number + 2]
    out_ref, joined, scratch = refs[number + 2], refs[number + 3 : -3], refs[-3:]
    planes = field_refs[0].shape[0]
    part = mine_ref.shape[1]
    core = core_ref[0]
    for i in range(number):
        joined[i][:planes] = field_refs[i][...]
        joined[i][pl.ds(planes + part * core, part)] = mine_ref[i]
        joined[i][pl.ds(planes + part * (1 - core), part)] = other_ref[i]
    cut_patches(count, corner_ref, factor_ref, order_ref, joined, *scratch, out_ref)


def in_cells(field):
    return field.reshape(field.shape[:-2] + (field.shape[-2] // 8, 8, LANES))


def join_and_cut(core, corner, factors, order, fields, mine, other):
    count = corner.shape[0]
    number = len(fields)
    fields = [in_cells(f) for f in fields]
    mine, other = in_cells(mine), in_cells(other)
    joined = (fields[0].shape[0] + 2 * mine.shape[1],) + fields[0].shape[1:]
    return pl.pallas_call(
        functools.partial(join_kernel, count, number),
        in_specs=[pl.BlockSpec(memory_space=SMEM)] * 3
        + [pl.BlockSpec(memory_space=VMEM)] * (number + 3),
        out_specs=[pl.BlockSpec(memory_space=VMEM)] * (number + 1),
        out_shape=[jax.ShapeDtypeStruct((count, TOK, VOX), BF16)]
        + [jax.ShapeDtypeStruct(joined, BF16)] * number,
        scratch_shapes=cut_scratch(count),
        compiler_params=PARAMS,
        cost_estimate=cost(4),
        name="join_and_cut",
    )(core, corner, factors, order, *fields, mine, other)


def cut_kernel(count, corner_ref, factor_ref, order_ref, *refs):
    fields, out_ref, scratch = refs[:2], refs[2], refs[3:]
    cut_patches(count, corner_ref, factor_ref, order_ref, fields, *scratch, out_ref)


def cut_tokens(corner, factors, order, clean, noisy):
    count = corner.shape[0]
    return pl.pallas_call(
        functools.partial(cut_kernel, count),
        in_specs=[pl.BlockSpec(memory_space=SMEM)] * 2 + [pl.BlockSpec(memory_space=VMEM)] * 3,
        out_specs=pl.BlockSpec(memory_space=VMEM),
        out_shape=jax.ShapeDtypeStruct((count, TOK, VOX), BF16),
        scratch_shapes=cut_scratch(count),
        compiler_params=PARAMS,
        cost_estimate=cost(7),
        name="cut_tokens",
    )(corner, factors, order, clean, noisy)


def place_kernel(corner_ref, core_ref, *refs):
    score_refs = refs[:PPD]
    same_ref, other_ref, buffer, work = refs[PPD:]
    lane = lax.broadcasted_iota(jnp.int32, (8, LANES), 1)
    wide = lax.broadcasted_iota(jnp.int32, (64, LANES), 1)
    buffer[...] = jnp.zeros_like(buffer)
    for number in range(PPD):
        z0 = corner_ref[number, 0]
        y0 = corner_ref[number, 1]
        x0 = corner_ref[number, 2]
        inside = (wide >= x0) & (wide < x0 + 64)
        for pz in range(PZT):
            for ez in range(0, EDGE, 2):
                tiles = [
                    score_refs[number][
                        px * 32 + pz * 8 : px * 32 + pz * 8 + 8,
                        (ez // 2) * LANES : (ez // 2 + 1) * LANES,
                    ].astype(F32)
                    for px in range(PXY)
                ]
                tiles = exchange_groups(tiles, lane)
                slot = pz * 4 + ez // 2
                for ey in range(8):
                    work[slot, pl.ds(ey, 8, stride=8), :] = tiles[ey]
                both = work[slot]
                for odd in range(2):
                    plane = pltpu.roll(both, lax.rem(LANES + x0 - 64 * odd, LANES), 1)
                    plane = jnp.where(inside, plane, 0.0).reshape(PXY, 8, LANES)
                    z = z0 + pz * EDGE + ez + odd
                    buffer[z, pl.ds(y0, PXY)] += plane
    cells = same_ref.shape[2]
    for i in range(same_ref.shape[1]):
        for ref, parity in ((same_ref, core_ref[0]), (other_ref, 1 - core_ref[0])):
            ref[:, i] = buffer[:, pl.ds((2 * i + parity) * cells, cells)].astype(BF16)


def place_scores(core, corner, members, scores, planes, rows):
    shape = (planes, rows // 8, 8, LANES)
    half = (planes, members // 2, rows // 8 // members, 8, LANES)
    outs = pl.pallas_call(
        place_kernel,
        in_specs=[pl.BlockSpec(memory_space=SMEM)] * 2 + [pl.BlockSpec(memory_space=VMEM)] * PPD,
        out_specs=[pl.BlockSpec(memory_space=VMEM)] * 2,
        out_shape=[jax.ShapeDtypeStruct(half, BF16)] * 2,
        scratch_shapes=[pltpu.VMEM(shape, F32), pltpu.VMEM((16, 64, LANES), F32)],
        compiler_params=PARAMS,
        cost_estimate=cost(6),
        name="place_scores",
    )(corner, core, *scores)
    return [out.reshape(planes, rows // 2, LANES) for out in outs]


def start_loads(refs, buffers, sems):
    copies = [
        pltpu.make_async_copy(ref, buffer, sems.at[i])
        for i, (ref, buffer) in enumerate(zip(refs, buffers))
    ]
    for copy in copies:
        copy.start()
    return copies


def finish(copies):
    for copy in copies:
        copy.wait()


def load_scratch(operands):
    return [pltpu.VMEM(x.shape, x.dtype) for x in operands] + [
        pltpu.SemaphoreType.DMA((len(operands),))
    ]


def member_blocks(pair_refs, other_ref):
    blocks = []
    for i, ref in enumerate(pair_refs):
        blocks += [ref.at[0], other_ref.at[i]]
    return blocks


def fold_kernel(pairs, me_ref, embed_ref, pos_ref, level_ref, *refs):
    blocks, out_ref = member_blocks(refs[:pairs], refs[pairs]), refs[pairs + 1]
    me = me_ref[0]
    width = embed_ref.shape[1]
    depth = width // len(blocks)
    start = 0
    column = jnp.zeros((1, HD), F32)
    for block in blocks:
        column += jnp.sum(block[...].astype(F32), axis=0, keepdims=True)
    for part in (embed_ref, pos_ref, level_ref):
        rows = part.shape[0]
        total = jnp.zeros((rows, HD), F32)
        for k, block in enumerate(blocks):
            at = pl.multiple_of(jnp.bitwise_xor(me, k) * depth, LANES)
            total += rows_dot(part[:, pl.ds(at, depth)], block[...])
        mean = jnp.sum(part[...].astype(F32), axis=1, keepdims=True) / width
        out_ref[start : start + rows, :] = (total - mean * column).astype(BF16)
        start += rows


def fold_weights(me, embed, pos, level, pairs, other):
    rows = embed.shape[0] + pos.shape[0] + level.shape[0]
    return pl.pallas_call(
        functools.partial(fold_kernel, len(pairs)),
        in_specs=[pl.BlockSpec(memory_space=SMEM)]
        + [pl.BlockSpec(memory_space=VMEM)] * 3
        + [pl.BlockSpec(memory_space=VMEM)] * (1 + len(pairs)),
        out_specs=pl.BlockSpec(memory_space=VMEM),
        out_shape=jax.ShapeDtypeStruct((rows, HD), BF16),
        compiler_params=PARAMS,
        cost_estimate=cost(2),
        name="fold_weights",
    )(me, embed, pos, level, *pairs, other)


def head_normal(values):
    inverse = lax.rsqrt(jnp.mean(values * values, axis=-1, keepdims=True) + 1e-06)
    return (values * inverse, inverse)


def project(info_ref, token_ref, fold_ref, work):
    count = token_ref.shape[0]
    patches = fold_ref.shape[1] - VOX - TOK
    tokens = token_ref[...].reshape(count * TOK, VOX)
    row = lax.broadcasted_iota(jnp.int32, (count * TOK, patches), 0) // TOK
    place = info_ref[1] + row * PPD
    onehot = (lax.broadcasted_iota(jnp.int32, (count * TOK, patches), 1) == place).astype(BF16)
    for kind in range(KINDS):
        fold = fold_ref.at[info_ref[2 + kind]]
        total = rows_dot(tokens, fold[:VOX]) + rows_dot(onehot, fold[VOX + TOK :])
        pos = fold[VOX : VOX + TOK].astype(F32)
        for i in range(count):
            work[i, :, kind * HD : (kind + 1) * HD] = total[i * TOK : (i + 1) * TOK] + pos
    return tokens, onehot


def attend(patch, k, scale_ref, work):
    scale = jnp.transpose(jnp.broadcast_to(scale_ref[k], (HD, TOK)))
    kinds = [work[patch, :, j * HD : (j + 1) * HD] * scale for j in range(KINDS)]
    query_n, query_r = head_normal(kinds[0])
    key_n, key_r = head_normal(kinds[1])
    query_b, key_b, value_b = (query_n.astype(BF16), key_n.astype(BF16), kinds[2].astype(BF16))
    expo = jnp.exp(last_dot(query_b, key_b) * (1.0 / HD**0.5))
    probs = expo / jnp.sum(expo, axis=-1, keepdims=True)
    return (scale, (query_n, query_r, query_b), (key_n, key_r, key_b), value_b, probs)


def forward_kernel(info_ref, token_ref, scale_ref, fold_ref, *refs):
    out_refs, work = refs[:-1], refs[-1]
    project(info_ref, token_ref, fold_ref, work)
    for k in range(token_ref.shape[0]):
        patch = jnp.bitwise_xor(info_ref[0], k)
        _, _, _, value_b, probs = attend(patch, k, scale_ref, work)
        out_refs[k // 2][k % 2] = rows_dot(probs.astype(BF16), value_b).astype(BF16)


def backward_kernel(last, pairs, info_ref, *refs):
    token_ref, scale_ref, fold_ref = refs[:3]
    refs = refs[3:]
    loads = pairs + 1 + last
    out_ref, work, grads = refs[loads : loads + 3]
    buffers, sems = refs[-loads - 1 : -1], refs[-1]
    copies = start_loads(refs[:loads], buffers, sems)
    blocks = member_blocks(buffers[:pairs], buffers[pairs])
    before_ref = buffers[-1] if last else None
    tokens, onehot = project(info_ref, token_ref, fold_ref, work)
    finish(copies)
    place_sum = jnp.zeros((TOK, KINDS * HD), F32)
    for k in range(token_ref.shape[0]):
        patch = jnp.bitwise_xor(info_ref[0], k)
        scale, query, key, value_b, probs = attend(patch, k, scale_ref, work)
        query_n, query_r, query_b = query
        key_n, key_r, key_b = key
        d_att = blocks[k][...]
        d_probs = last_dot(d_att, value_b)
        d_value = first_dot(probs.astype(BF16), d_att)
        row_total = jnp.sum(d_probs * probs, axis=-1, keepdims=True)
        d_logits = (probs * (d_probs - row_total) * (1.0 / HD**0.5)).astype(BF16)
        d_query_n = rows_dot(d_logits, key_b)
        d_key_n = first_dot(d_logits, query_b)
        d_query = query_r * (
            d_query_n - query_n * jnp.mean(d_query_n * query_n, axis=-1, keepdims=True)
        )
        d_key = key_r * (d_key_n - key_n * jnp.mean(d_key_n * key_n, axis=-1, keepdims=True))
        grad = jnp.concatenate([d_query * scale, d_key * scale, d_value * scale], axis=1)
        place_sum += grad
        grads[pl.ds(pl.multiple_of(patch * TOK, TOK), TOK), :] = grad.astype(BF16)
    all_grads = grads[...]
    parts = (first_dot(tokens, all_grads), place_sum, first_dot(onehot, all_grads))
    start = 0
    for part in parts:
        rows = part.shape[0]
        for kind in range(KINDS):
            block = part[:, kind * HD : (kind + 1) * HD]
            if last:
                block += before_ref[kind, start : start + rows]
            out_ref[kind, start : start + rows] = block.astype(out_ref.dtype)
        start += rows


def forward_heads(info, tokens, scale, folds):
    heads = scale.shape[0]
    return pl.pallas_call(
        forward_kernel,
        in_specs=[pl.BlockSpec(memory_space=SMEM)] + [pl.BlockSpec(memory_space=VMEM)] * 3,
        out_specs=[pl.BlockSpec(memory_space=VMEM)] * (heads // 2),
        out_shape=[jax.ShapeDtypeStruct((2, TOK, HD), BF16)] * (heads // 2),
        scratch_shapes=[pltpu.VMEM((heads, TOK, KINDS * HD), F32)],
        compiler_params=PARAMS,
        cost_estimate=cost(5),
        name="forward_heads",
    )(info, tokens, scale, folds)


def backward_heads(info, tokens, scale, folds, pairs, other, before):
    heads = scale.shape[0]
    last = before is not None
    operands = [*pairs, other] + ([before] if last else [])
    return pl.pallas_call(
        functools.partial(backward_kernel, last, len(pairs)),
        in_specs=[pl.BlockSpec(memory_space=SMEM)]
        + [pl.BlockSpec(memory_space=VMEM)] * 3
        + [pl.BlockSpec(memory_space=HBM)] * len(operands),
        out_specs=pl.BlockSpec(memory_space=VMEM),
        out_shape=jax.ShapeDtypeStruct((KINDS,) + folds.shape[1:], BF16 if last else F32),
        scratch_shapes=[
            pltpu.VMEM((heads, TOK, KINDS * HD), F32),
            pltpu.VMEM((heads * TOK, KINDS * HD), BF16),
        ]
        + load_scratch(operands),
        compiler_params=pltpu.CompilerParams(vmem_limit_bytes=28 * 1024 * 1024),
        cost_estimate=cost(9),
        name="backward_heads",
    )(info, tokens, scale, folds, *operands)


def output_kernel(pairs, me_ref, *refs):
    loads = pairs + 5
    operands, outs = refs[:loads], refs[loads : loads + 4 + pairs]
    work, buffers, sems = refs[loads + 4 + pairs], refs[-loads - 1 : -1], refs[-1]
    copies = start_loads(operands, buffers, sems)
    cot_ref, unembed_ref, hidden_ref, w_ref = buffers[:4]
    blocks = member_blocks(buffers[4:-1], buffers[-1])
    score_ref, same_ref, other_ref, d_hidden_ref = outs[:4]
    d_att_refs = outs[4:]
    me = me_ref[0]
    finish(copies[:2])
    d_feat = last_dot(cot_ref[...], unembed_ref[...])
    finish(copies[2:])
    for k, block in enumerate(blocks):
        at = pl.multiple_of(jnp.bitwise_xor(me, k) * HD, HD)
        work[:, pl.ds(at, HD)] = block[...]
        at = pl.multiple_of(jnp.bitwise_xor(me, k) // 2 * HD, HD)
        (other_ref if k % 2 else same_ref)[:, pl.ds(at, HD)] = block[...]
    hidden = hidden_ref[...] + rows_dot(work[...], w_ref[...])
    centre = hidden - jnp.mean(hidden, axis=-1, keepdims=True)
    inverse = lax.rsqrt(jnp.mean(centre * centre, axis=-1, keepdims=True) + 1e-05)
    feat = centre * inverse
    score_ref[...] = rows_dot(feat.astype(BF16), unembed_ref[...])
    d_hidden = inverse * (
        d_feat
        - jnp.mean(d_feat, axis=-1, keepdims=True)
        - feat * jnp.mean(d_feat * feat, axis=-1, keepdims=True)
    )
    d_hidden = d_hidden.astype(BF16)
    d_hidden_ref[...] = d_hidden
    work[...] = last_dot(d_hidden, w_ref[...]).astype(BF16)
    for k in range(len(blocks)):
        at = pl.multiple_of(jnp.bitwise_xor(me, k) * HD, HD)
        d_att_refs[k // 2][k % 2] = work[:, pl.ds(at, HD)]


def output_part(me, hidden, cot, w_out, unembed, pairs, other):
    inner, width = w_out.shape
    operands = [cot, unembed, hidden, w_out, *pairs, other]
    shape = jax.ShapeDtypeStruct
    return pl.pallas_call(
        functools.partial(output_kernel, len(pairs)),
        in_specs=[pl.BlockSpec(memory_space=SMEM)]
        + [pl.BlockSpec(memory_space=HBM)] * len(operands),
        out_specs=[pl.BlockSpec(memory_space=VMEM)] * (4 + len(pairs)),
        out_shape=[
            shape((TOK, VOX), F32),
            shape((TOK, inner // 2), BF16),
            shape((TOK, inner // 2), BF16),
            shape((TOK, width), BF16),
        ]
        + [shape((2, TOK, HD), BF16)] * len(pairs),
        scratch_shapes=[pltpu.VMEM((TOK, inner), BF16)] + load_scratch(operands),
        compiler_params=pltpu.CompilerParams(vmem_limit_bytes=32 * 1024 * 1024),
        cost_estimate=cost(8),
        name="output_part",
    )(me, *operands)


def expand_kernel(heads, number, me_ref, embed_ref, pos_ref, level_ref, own_ref, *refs):
    in_refs, out_refs, work = refs[:number], refs[number:-1], refs[-1]
    total = own_ref[...].astype(F32)
    for ref in in_refs:
        total += ref[...].astype(F32)
    total = total.astype(BF16)
    split = embed_ref.shape[0]
    after = split + pos_ref.shape[0]
    grad = first_dot(embed_ref[...], total[:split])
    grad += first_dot(pos_ref[...], total[split:after])
    grad += first_dot(level_ref[...], total[after:])
    grad -= jnp.mean(grad, axis=0, keepdims=True)
    work[...] = grad.astype(BF16)
    depth = out_refs[0].shape[1]
    base = (me_ref[0] // heads) * heads
    for k in range(heads):
        member = base + jnp.bitwise_xor(lax.rem(me_ref[0], heads), k)
        at = pl.multiple_of(member * depth, depth)
        out_refs[k // 2][k % 2] = work[pl.ds(at, depth), :]


def expand_sums(me, heads, depth, embed, pos, level, own, others):
    width = embed.shape[1]
    columns = own.shape[1]
    return pl.pallas_call(
        functools.partial(expand_kernel, heads, len(others)),
        in_specs=[pl.BlockSpec(memory_space=SMEM)]
        + [pl.BlockSpec(memory_space=VMEM)] * 3
        + [pl.BlockSpec(memory_space=VMEM)] * (1 + len(others)),
        out_specs=[pl.BlockSpec(memory_space=VMEM)] * (heads // 2),
        out_shape=[jax.ShapeDtypeStruct((2, depth, columns), BF16)] * (heads // 2),
        scratch_shapes=[pltpu.VMEM((width, columns), BF16)],
        compiler_params=PARAMS,
        cost_estimate=cost(2),
        name="expand_sums",
    )(me, embed, pos, level, own, *others)


def on_device(
    slabs,
    members,
    volume,
    noise,
    cotangent,
    patch_corner,
    patch_count,
    patch_level,
    embed,
    unembed,
    level_table,
    pos_embed,
    w_qkv,
    w_out,
):
    planes, side = volume.shape[:2]
    width = embed.shape[1]
    inner = w_out.shape[0] * members
    heads = inner // HD
    groups = members // heads
    depth = w_qkv.shape[0]
    slab = lax.axis_index("slab")
    member = lax.axis_index("fsdp")
    group, head = member // heads, member % heads

    def in_group(block, k):
        pairs = [(i, (i // heads) * heads + ((i % heads) ^ k)) for i in range(members)]
        return swap(block, "fsdp", pairs)

    def among_slabs(block, k):
        return across(block, "slab", slabs, k)

    def to_chips(pairs, move):
        return [move(pair, 2 * i) if i else pair for i, pair in enumerate(pairs)]

    def for_cores(landed):
        return jnp.stack([pair[1] for pair in landed])

    me = jnp.reshape(member, (1,)).astype(jnp.int32)
    core = member % 2

    part = HALO // 2

    def rims_of(*fields):
        rims = jnp.stack(
            [lax.dynamic_slice(f, (core * part, 0, 0), (part, side, side)) for f in fields]
        )
        rims = swap(rims, "slab", [(i, i - 1) for i in range(1, slabs)])
        return rims, across(rims, "fsdp", members, 1)

    rims, other_rims = rims_of(volume, noise)

    total = members * PPD
    all_corner, all_level = pick_patches(
        patch_count[0], patch_corner[0], patch_level[0], 0, total
    )
    group_first = group * heads * PPD
    corner = lax.dynamic_slice(all_corner, (group_first, 0), (heads * PPD, 3))
    level = lax.dynamic_slice(all_level, (group_first,), (heads * PPD,))
    corner = jnp.stack([corner[:, 0] - slab * planes, corner[:, 1] // 8, corner[:, 2]], axis=1)
    own_corner = lax.dynamic_slice(corner, (head * PPD, 0), (PPD, 3))
    levels = jnp.stack([among_slabs(all_level, k) if k else all_level for k in range(slabs)])
    w_qkv = after(w_qkv, levels)
    levels = jnp.take(levels, jnp.arange(slabs, dtype=jnp.int32) ^ slab, axis=0).reshape(-1)

    kind = slab % KINDS
    w_pairs = []
    for k in range(0, members, 2):
        pair = [
            lax.dynamic_slice(
                w_qkv, (0, kind * inner + ((member ^ (k + j)) % heads) * HD), (depth, HD)
            )
            for j in range(2)
        ]
        w_pairs.append(jnp.stack(pair))
    w_pairs = to_chips(w_pairs, lambda x, k: across(x, "fsdp", members, k))

    onehot = (levels[:, None] == jnp.arange(level_table.shape[0], dtype=jnp.int32)[None, :]).astype(
        BF16
    )
    level_rows = jnp.dot(onehot, level_table, preferred_element_type=F32).astype(BF16)

    pos = pos_embed.reshape(PZT * PXY, PXY, width).transpose(1, 0, 2).reshape(TOK, width)

    factors = jnp.stack(noise_factors(level), axis=1)
    own_factors = lax.dynamic_slice(factors, (head * PPD, 0), (PPD, 2))
    core_of = jnp.reshape(core, (1,)).astype(jnp.int32)
    order = lane_order()
    own_tokens, clean, noisy = join_and_cut(
        core_of, own_corner, own_factors, order, (volume, noise), rims, other_rims
    )
    own_place = slab * total + member * PPD
    own_rows = lax.dynamic_slice(level_rows, (own_place, 0), (PPD, width)).astype(F32)
    hidden = jnp.dot(own_tokens.reshape(PPD * TOK, VOX), embed, preferred_element_type=F32)
    hidden = hidden.reshape(PPD, TOK, width) + own_rows[:, None, :] + pos.astype(F32)[None]
    centre = hidden - jnp.mean(hidden, axis=-1, keepdims=True)
    scale = lax.rsqrt(jnp.mean(centre * centre, axis=-1) + 1e-05)[None]
    scale = scale.astype(F32)
    w_out = after(w_out, w_pairs)
    w_pairs = after(w_pairs, scale)
    w_other = across(for_cores(w_pairs), "fsdp", members, 1)
    clean, noisy = after((clean, noisy), w_pairs)
    tokens = [cut_tokens(corner[::PPD], factors[::PPD], order, clean, noisy)]
    w_pairs, w_other = after((w_pairs, w_other), tokens)
    fold = fold_weights(me, embed, pos, level_rows, w_pairs, w_other)
    folds = jnp.stack([among_slabs(fold, k) if k else fold for k in range(slabs)])
    clean, noisy = after((clean, noisy), fold)
    tokens += [
        cut_tokens(corner[n::PPD], factors[n::PPD], order, clean, noisy) for n in range(1, PPD)
    ]
    step = 1
    while step < heads:
        scale = jnp.concatenate([scale, in_group(scale, step)], axis=0)
        step *= 2
    scales = [scale[:, n].reshape(heads, 1, TOK) for n in range(PPD)]

    tangents, _ = join_and_cut(
        core_of, own_corner, own_factors, order, (cotangent,), *rims_of(after(cotangent, folds))
    )
    full_out = lax.all_gather(w_out, "fsdp", axis=0, tiled=True)

    infos = [
        jnp.stack([head, slab * total + group_first + n] + [slab ^ j for j in range(KINDS)]).astype(
            jnp.int32
        )
        for n in range(PPD)
    ]
    head_me = jnp.reshape(head, (1,)).astype(jnp.int32)
    def output_of(n, landed, other):
        score, same, diff, d_hidden, *d_att = output_part(
            head_me, hidden[n], tangents[n], full_out, unembed, landed, other
        )
        return (score, same, diff, d_hidden), d_att

    results, sends, returns = [], [], []
    att = forward_heads(infos[0], tokens[0], scales[0], folds)
    landed = to_chips(att, in_group)
    for n in range(PPD):
        crossing = for_cores(landed)
        if returns:
            returns = to_chips(after(returns, crossing), in_group)
            sends.append(returns)
        if n + 1 < PPD:
            att = forward_heads(infos[n + 1], tokens[n + 1], scales[n + 1], folds)
            coming = to_chips(after(att, crossing), in_group)
        result, returns = output_of(n, landed, in_group(crossing, 1))
        results.append(result)
        if n + 1 < PPD:
            landed = after(coming, returns)
    scores, sames, diffs, d_hiddens = zip(*results)
    crossing = for_cores(after(sends[0], returns))
    sends.append(to_chips(after(returns, crossing), in_group))
    sames, diffs, d_hiddens = after((sames, diffs, d_hiddens), crossing)

    d_hidden = jnp.concatenate(d_hiddens, axis=0)
    away = first_dot(jnp.concatenate(diffs, axis=0), d_hidden).astype(BF16)
    if groups == 1:
        away = across(away, "fsdp", members, 1)

    sums = backward_heads(
        infos[0], tokens[0], scales[0], folds, sends[0], in_group(crossing, 1), None
    )
    crossing = for_cores(after(sends[1], sums))
    stay = first_dot(
        jnp.concatenate(sames, axis=0), after(d_hidden, crossing)
    )
    if groups > 1:
        both = [stay.astype(BF16).reshape(-1, HD, width), away.reshape(-1, HD, width)]
        even = jnp.where(core == 0, both[0], both[1])
        odd = jnp.where(core == 0, both[1], both[0])
        out_sum = jnp.stack([even, odd], axis=1).reshape(inner, width)
    else:
        out_sum = (stay + away.astype(F32)).astype(BF16)
    columns = width // slabs

    def for_slab(k):
        return lax.dynamic_slice(out_sum, (0, (slab ^ k) * columns), (out_sum.shape[0], columns))

    slab_parts = [among_slabs(for_slab(k), k) for k in range(1, slabs)]

    near, far = place_scores(
        core_of, own_corner, members, after(scores, crossing), planes + HALO, side
    )
    far = across(far, "fsdp", members, 1)

    before, pairs, other = after((sums, sends[1], in_group(crossing, 1)), near, out_sum)
    sums = backward_heads(infos[1], tokens[1], scales[1], folds, pairs, other, before)

    half = slabs // 2

    def sums_for(target):
        qk = lax.dynamic_index_in_dim(sums, target // half, 0, keepdims=False)
        return jnp.concatenate([qk, sums[2]], axis=1)

    qk_heads = heads // half
    v_heads = heads // slabs

    def owns(s, h):
        return (h // qk_heads == s % half, h // v_heads == s)

    def to_owner(k):
        pairs = [
            (s * members + i, (s ^ k) * members + i)
            for s in range(slabs)
            for i in range(members)
            if any(owns(s ^ k, i % heads))
        ]
        return swap(sums_for(slab ^ k), ("slab", "fsdp"), pairs)

    slab_sum = for_slab(0).astype(F32)
    for block in slab_parts:
        slab_sum += block.astype(F32)
    slab_sum = slab_sum.astype(BF16)
    sums = after(sums, slab_sum)
    others = [to_owner(k) for k in range(1, slabs)]
    chip = (near.astype(F32) + far.astype(F32)).astype(BF16)
    lines = side // members
    depth_out = slab_sum.shape[0] // (members // 2)
    rows_score = (planes + HALO) * lines * side // LANES

    def for_chip(k):
        at = (member ^ k) // 2
        part = lax.dynamic_slice(chip, (0, at * lines, 0), (planes + HALO, lines, side))
        part = part.reshape(rows_score, LANES)
        if groups > 1:
            return part
        block = lax.dynamic_slice(slab_sum, (at * depth_out, 0), (depth_out, columns))
        return jnp.concatenate([part] + jnp.split(block, columns // LANES, axis=1), axis=0)

    chip_sends = [for_chip(k) for k in range(2, members, 2)]
    others = after(others, chip_sends)
    chip_sum = for_chip(0).astype(F32)
    for i, send in enumerate(chip_sends):
        chip_sum += across(send, "fsdp", members, 2 * i + 2).astype(F32)
    summed = chip_sum[:rows_score].reshape(planes + HALO, lines, side)
    if groups > 1:
        grad_out = lax.psum_scatter(slab_sum, "fsdp", scatter_dimension=0, tiled=True).astype(F32)
    else:
        grad_out = chip_sum[rows_score:].reshape(columns // LANES, depth_out, LANES)
        grad_out = grad_out.transpose(1, 0, 2).reshape(depth_out, columns)
    own = sums_for(slab)
    if groups > 1:
        gathered = own.astype(F32)
        for block in others:
            gathered += block.astype(F32)
        own = gathered.astype(BF16)
        others = []
        for g in range(1, groups):
            route = [(i, ((i // heads) ^ g) * heads + i % heads) for i in range(members)]
            others.append(swap(own, "fsdp", route))
    blocks = expand_sums(me, heads, depth, embed, pos, level_rows, own, others)
    pairs_of = []
    for k in range(heads):
        pairs = []
        for s in range(slabs):
            for i in range(members):
                h = i % heads
                if any(owns(s, h)):
                    j = (i // heads) * heads + (h ^ k)
                    pairs.append((s * members + i, s * members + j))
        pairs_of.append(pairs)
    arrived = to_chips(blocks, lambda x, k: swap(x, ("slab", "fsdp"), pairs_of[k]))
    arrived_other = in_group(for_cores(arrived), 1)
    arrived = jnp.stack([pair[0] for pair in arrived])
    arrived = jnp.stack([arrived, arrived_other], axis=1).reshape(heads, depth, 2 * HD)

    def from_heads(first, number, column):
        pieces = [
            lax.dynamic_index_in_dim(arrived, head ^ (first + i), 0, keepdims=False)[
                :, column * HD : (column + 1) * HD
            ]
            for i in range(number)
        ]
        return jnp.concatenate(pieces, axis=1).astype(F32)

    grad_qk = from_heads((slab % half) * qk_heads, qk_heads, 0)
    grad_v = from_heads(slab * v_heads, v_heads, 1)

    rim = summed[planes:].astype(BF16)
    arrived_rim = swap(rim, "slab", [(i, i + 1) for i in range(slabs - 1)])
    score = summed[:planes].at[:HALO].add(arrived_rim.astype(F32))
    return (score, grad_qk, grad_v, grad_out)


def solution(mesh):
    placed = (
        P("slab", None, None),
        P("slab", None, None),
        P("slab", None, None),
        P("slab", None, None),
        P("slab", None),
        P("slab", None),
        P(),
        P(),
        P(),
        P(),
        P("fsdp", None),
        P("fsdp", None),
    )
    return jax.shard_map(
        functools.partial(on_device, mesh.shape["slab"], mesh.shape["fsdp"]),
        mesh=mesh,
        in_specs=placed,
        out_specs=(
            P("slab", "fsdp", None),
            P("fsdp", "slab"),
            P("fsdp", "slab"),
            P("fsdp", "slab"),
        ),
        check_vma=False,
    )
```

```python
import functools

import jax
import jax.numpy as jnp
from jax import lax
from jax.experimental import pallas as pl
from jax.experimental.pallas import tpu as pltpu
from jax.sharding import PartitionSpec as P

HD = 128
NLEV = 1000
EDGE = 8
PXY = 8
PZT = 4
PPD = 2
HALO = 24
TOK = PZT * PXY * PXY
VOX = EDGE * EDGE * EDGE
KINDS = 3
LANES = 128

F32 = jnp.float32
BF16 = jnp.bfloat16
VMEM = pltpu.MemorySpace.VMEM
SMEM = pltpu.MemorySpace.SMEM
HBM = pltpu.MemorySpace.HBM
PARAMS = pltpu.CompilerParams(vmem_limit_bytes=20 * 1024 * 1024)


def cost(microseconds):
    return pl.CostEstimate(
        flops=int(microseconds * 1e9), bytes_accessed=1 << 20, transcendentals=0
    )


def swap(block, axis, pairs):
    return lax.ppermute(block, axis, pairs)


def after(value, *others):
    return lax.optimization_barrier((value, others))[0]


def across(block, axis, size, k):
    return lax.ppermute(block, axis, [(i, i ^ k) for i in range(size)])


def rows_dot(left, right):
    return lax.dot_general(left, right, (((1,), (0,)), ((), ())), preferred_element_type=F32)


def last_dot(left, right):
    return lax.dot_general(left, right, (((1,), (1,)), ((), ())), preferred_element_type=F32)


def first_dot(left, right):
    return lax.dot_general(left, right, (((0,), (0,)), ((), ())), preferred_element_type=F32)


def pick_patches(counts, corners, levels, first, number):
    slots = corners.shape[0] // counts.shape[0]
    live = (
        (jnp.arange(slots, dtype=jnp.int32)[None, :] < counts[:, None])
        .reshape(-1)
        .astype(jnp.int32)
    )
    before = jnp.cumsum(live, dtype=jnp.int32) - live
    wanted = first + jnp.arange(number, dtype=jnp.int32)
    chosen = ((before[None, :] == wanted[:, None]) & (live[None, :] == 1)).astype(jnp.int32)
    chosen_corner = jnp.sum(chosen[:, :, None] * corners[None, :, :], axis=1, dtype=jnp.int32)
    chosen_level = jnp.sum(chosen * levels[None, :], axis=1, dtype=jnp.int32)
    return (chosen_corner, chosen_level)


def noise_factors(chosen_level):
    sigma_level = 0.5 * jnp.exp(jnp.log(8.0) * chosen_level.astype(F32) / (NLEV - 1))
    return (sigma_level, lax.rsqrt(1.0 + sigma_level * sigma_level))


def exchange_groups(tiles, lane):
    for bit in range(3):
        step = 1 << bit
        upper = ((lane >> (3 + bit)) & 1) == 1
        fresh = []
        for i in range(8):
            other = tiles[i ^ step]
            if i & step:
                moved = pltpu.roll(other, LANES - 8 * step, 1)
                fresh.append(jnp.where(upper, tiles[i], moved))
            else:
                moved = pltpu.roll(other, 8 * step, 1)
                fresh.append(jnp.where(upper, moved, tiles[i]))
        tiles = fresh
    return tiles


def lane_order():
    row = lax.broadcasted_iota(jnp.int32, (8 * LANES, 8 * LANES), 0)
    lane = lax.broadcasted_iota(jnp.int32, (8 * LANES, 8 * LANES), 1)
    source = (lane // 8) % 8 * LANES + (lane // 64) % 2 * 64 + lane // LANES * 8 + lane % 8
    return (row == source).astype(BF16)


def cut_patches(count, corner_ref, factor_ref, order_ref, fields, pairs, work, wide, out_ref):
    row = lax.broadcasted_iota(jnp.int32, (2 * LANES, LANES), 0)
    lane = lax.broadcasted_iota(jnp.int32, (2 * LANES, LANES), 1)
    source = lane // 64 * LANES + lane % 64

    def body(number, carry):
        z0 = corner_ref[number, 0]
        y0 = corner_ref[number, 1]
        for pz in range(PZT):
            for ez in range(EDGE):
                z = z0 + pz * EDGE + ez
                plane = fields[0][z, pl.ds(y0, PXY)].astype(F32)
                if len(fields) == 2:
                    noise = fields[1][z, pl.ds(y0, PXY)].astype(F32)
                    plane = (plane + factor_ref[number, 0] * noise) * factor_ref[number, 1]
                at = (pz * 4 + ez // 2) * 64
                half = ez % 2 * LANES
                pairs[at : at + 64, half : half + LANES] = plane.reshape(64, LANES).astype(BF16)
        select = (row == source + corner_ref[number, 2]).astype(BF16)
        work[...] = rows_dot(pairs[...], select)
        at = pl.multiple_of(number * LANES, LANES)
        for ey in range(EDGE):
            tile = work[pl.ds(ey, LANES, stride=8), :]
            wide[pl.ds(at, LANES), ey * LANES : (ey + 1) * LANES] = tile.astype(BF16)
        return carry

    lax.fori_loop(0, count, body, 0)
    for two in range(PXY // 2):
        moved = rows_dot(wide[...], order_ref[:, two * 2 * LANES : (two + 1) * 2 * LANES])
        for number in range(count):
            for pair in range(PZT // 2):
                for ez in range(EDGE // 2):
                    first = number * LANES + (2 * pair * 4 + ez) * 8
                    second = first + 4 * 8
                    both = jnp.concatenate(
                        [moved[first : first + 8], moved[second : second + 8]], axis=0
                    ).astype(BF16)
                    for px in range(2):
                        at = (two * 2 + px) * 32 + pair * 16
                        out_ref[number, at : at + 16, ez * LANES : (ez + 1) * LANES] = both[
                            :, px * LANES : (px + 1) * LANES
                        ]


def cut_scratch(count):
    return [
        pltpu.VMEM((16 * 64, 2 * LANES), BF16),
        pltpu.VMEM((16 * 64, LANES), F32),
        pltpu.VMEM((count * LANES, 8 * LANES), BF16),
    ]


def join_kernel(count, number, core_ref, corner_ref, factor_ref, order_ref, *refs):
    field_refs, (mine_ref, other_ref) = refs[:number], refs[number : number + 2]
    out_ref, joined, scratch = refs[number + 2], refs[number + 3 : -3], refs[-3:]
    planes = field_refs[0].shape[0]
    part = mine_ref.shape[1]
    core = core_ref[0]
    for i in range(number):
        joined[i][:planes] = field_refs[i][...]
        joined[i][pl.ds(planes + part * core, part)] = mine_ref[i]
        joined[i][pl.ds(planes + part * (1 - core), part)] = other_ref[i]
    cut_patches(count, corner_ref, factor_ref, order_ref, joined, *scratch, out_ref)


def in_cells(field):
    return field.reshape(field.shape[:-2] + (field.shape[-2] // 8, 8, LANES))


def join_and_cut(core, corner, factors, order, fields, mine, other):
    count = corner.shape[0]
    number = len(fields)
    fields = [in_cells(f) for f in fields]
    mine, other = in_cells(mine), in_cells(other)
    joined = (fields[0].shape[0] + 2 * mine.shape[1],) + fields[0].shape[1:]
    return pl.pallas_call(
        functools.partial(join_kernel, count, number),
        in_specs=[pl.BlockSpec(memory_space=SMEM)] * 3
        + [pl.BlockSpec(memory_space=VMEM)] * (number + 3),
        out_specs=[pl.BlockSpec(memory_space=VMEM)] * (number + 1),
        out_shape=[jax.ShapeDtypeStruct((count, TOK, VOX), BF16)]
        + [jax.ShapeDtypeStruct(joined, BF16)] * number,
        scratch_shapes=cut_scratch(count),
        compiler_params=PARAMS,
        cost_estimate=cost(4),
        name="join_and_cut",
    )(core, corner, factors, order, *fields, mine, other)


def cut_kernel(count, corner_ref, factor_ref, order_ref, *refs):
    fields, out_ref, scratch = refs[:2], refs[2], refs[3:]
    cut_patches(count, corner_ref, factor_ref, order_ref, fields, *scratch, out_ref)


def cut_tokens(corner, factors, order, clean, noisy):
    count = corner.shape[0]
    return pl.pallas_call(
        functools.partial(cut_kernel, count),
        in_specs=[pl.BlockSpec(memory_space=SMEM)] * 2 + [pl.BlockSpec(memory_space=VMEM)] * 3,
        out_specs=pl.BlockSpec(memory_space=VMEM),
        out_shape=jax.ShapeDtypeStruct((count, TOK, VOX), BF16),
        scratch_shapes=cut_scratch(count),
        compiler_params=PARAMS,
        cost_estimate=cost(7),
        name="cut_tokens",
    )(corner, factors, order, clean, noisy)


def place_kernel(corner_ref, *refs):
    score_refs = refs[:PPD]
    out_ref, buffer, work = refs[PPD:]
    lane = lax.broadcasted_iota(jnp.int32, (8, LANES), 1)
    wide = lax.broadcasted_iota(jnp.int32, (64, LANES), 1)
    buffer[...] = jnp.zeros_like(buffer)
    for number in range(PPD):
        z0 = corner_ref[number, 0]
        y0 = corner_ref[number, 1]
        x0 = corner_ref[number, 2]
        inside = (wide >= x0) & (wide < x0 + 64)
        for pz in range(PZT):
            for ez in range(0, EDGE, 2):
                tiles = [
                    score_refs[number][
                        px * 32 + pz * 8 : px * 32 + pz * 8 + 8,
                        (ez // 2) * LANES : (ez // 2 + 1) * LANES,
                    ].astype(F32)
                    for px in range(PXY)
                ]
                tiles = exchange_groups(tiles, lane)
                slot = pz * 4 + ez // 2
                for ey in range(8):
                    work[slot, pl.ds(ey, 8, stride=8), :] = tiles[ey]
                both = work[slot]
                for odd in range(2):
                    plane = pltpu.roll(both, lax.rem(LANES + x0 - 64 * odd, LANES), 1)
                    plane = jnp.where(inside, plane, 0.0).reshape(PXY, 8, LANES)
                    z = z0 + pz * EDGE + ez + odd
                    buffer[z, pl.ds(y0, PXY)] += plane
    out_ref[...] = buffer[...].astype(BF16)


def place_scores(corner, scores, planes, rows):
    shape = (planes, rows // 8, 8, LANES)
    out = pl.pallas_call(
        place_kernel,
        in_specs=[pl.BlockSpec(memory_space=SMEM)] + [pl.BlockSpec(memory_space=VMEM)] * PPD,
        out_specs=pl.BlockSpec(memory_space=VMEM),
        out_shape=jax.ShapeDtypeStruct(shape, BF16),
        scratch_shapes=[pltpu.VMEM(shape, F32), pltpu.VMEM((16, 64, LANES), F32)],
        compiler_params=PARAMS,
        cost_estimate=cost(6),
        name="place_scores",
    )(corner, *scores)
    return out.reshape(planes, rows, LANES)


def start_loads(refs, buffers, sems):
    copies = [
        pltpu.make_async_copy(ref, buffer, sems.at[i])
        for i, (ref, buffer) in enumerate(zip(refs, buffers))
    ]
    for copy in copies:
        copy.start()
    return copies


def finish(copies):
    for copy in copies:
        copy.wait()


def load_scratch(operands):
    return [pltpu.VMEM(x.shape, x.dtype) for x in operands] + [
        pltpu.SemaphoreType.DMA((len(operands),))
    ]


def member_blocks(pair_refs, other_ref):
    blocks = []
    for i, ref in enumerate(pair_refs):
        blocks += [ref.at[0], other_ref.at[i]]
    return blocks


def pack_kernel(*refs):
    for i, ref in enumerate(refs[:-1]):
        refs[-1][i] = ref[1]


def pack_seconds(pairs):
    return pl.pallas_call(
        pack_kernel,
        in_specs=[pl.BlockSpec(memory_space=VMEM)] * len(pairs),
        out_specs=pl.BlockSpec(memory_space=VMEM),
        out_shape=jax.ShapeDtypeStruct((len(pairs),) + pairs[0].shape[1:], pairs[0].dtype),
        cost_estimate=cost(1),
        name="pack_seconds",
    )(*pairs)


def fold_kernel(pairs, me_ref, embed_ref, pos_ref, level_ref, *refs):
    blocks, out_ref = member_blocks(refs[:pairs], refs[pairs]), refs[pairs + 1]
    me = me_ref[0]
    width = embed_ref.shape[1]
    depth = width // len(blocks)
    start = 0
    column = jnp.zeros((1, HD), F32)
    for block in blocks:
        column += jnp.sum(block[...].astype(F32), axis=0, keepdims=True)
    for part in (embed_ref, pos_ref, level_ref):
        rows = part.shape[0]
        total = jnp.zeros((rows, HD), F32)
        for k, block in enumerate(blocks):
            at = pl.multiple_of(jnp.bitwise_xor(me, k) * depth, LANES)
            total += rows_dot(part[:, pl.ds(at, depth)], block[...])
        mean = jnp.sum(part[...].astype(F32), axis=1, keepdims=True) / width
        out_ref[start : start + rows, :] = (total - mean * column).astype(BF16)
        start += rows


def fold_weights(me, embed, pos, level, pairs, other):
    rows = embed.shape[0] + pos.shape[0] + level.shape[0]
    return pl.pallas_call(
        functools.partial(fold_kernel, len(pairs)),
        in_specs=[pl.BlockSpec(memory_space=SMEM)]
        + [pl.BlockSpec(memory_space=VMEM)] * 3
        + [pl.BlockSpec(memory_space=VMEM)] * (1 + len(pairs)),
        out_specs=pl.BlockSpec(memory_space=VMEM),
        out_shape=jax.ShapeDtypeStruct((rows, HD), BF16),
        compiler_params=PARAMS,
        cost_estimate=cost(2),
        name="fold_weights",
    )(me, embed, pos, level, *pairs, other)


def head_normal(values):
    inverse = lax.rsqrt(jnp.mean(values * values, axis=-1, keepdims=True) + 1e-06)
    return (values * inverse, inverse)


def project(info_ref, token_ref, fold_ref, work):
    count = token_ref.shape[0]
    patches = fold_ref.shape[1] - VOX - TOK
    tokens = token_ref[...].reshape(count * TOK, VOX)
    row = lax.broadcasted_iota(jnp.int32, (count * TOK, patches), 0) // TOK
    place = info_ref[1] + row * PPD
    onehot = (lax.broadcasted_iota(jnp.int32, (count * TOK, patches), 1) == place).astype(BF16)
    for kind in range(KINDS):
        fold = fold_ref.at[info_ref[2 + kind]]
        total = rows_dot(tokens, fold[:VOX]) + rows_dot(onehot, fold[VOX + TOK :])
        pos = fold[VOX : VOX + TOK].astype(F32)
        for i in range(count):
            work[i, :, kind * HD : (kind + 1) * HD] = total[i * TOK : (i + 1) * TOK] + pos
    return tokens, onehot


def attend(patch, k, scale_ref, work):
    scale = jnp.transpose(jnp.broadcast_to(scale_ref[k], (HD, TOK)))
    kinds = [work[patch, :, j * HD : (j + 1) * HD] * scale for j in range(KINDS)]
    query_n, query_r = head_normal(kinds[0])
    key_n, key_r = head_normal(kinds[1])
    query_b, key_b, value_b = (query_n.astype(BF16), key_n.astype(BF16), kinds[2].astype(BF16))
    expo = jnp.exp(last_dot(query_b, key_b) * (1.0 / HD**0.5))
    probs = expo / jnp.sum(expo, axis=-1, keepdims=True)
    return (scale, (query_n, query_r, query_b), (key_n, key_r, key_b), value_b, probs)


def forward_kernel(info_ref, token_ref, scale_ref, fold_ref, *refs):
    out_refs, work = refs[:-1], refs[-1]
    project(info_ref, token_ref, fold_ref, work)
    for k in range(token_ref.shape[0]):
        patch = jnp.bitwise_xor(info_ref[0], k)
        _, _, _, value_b, probs = attend(patch, k, scale_ref, work)
        out_refs[k // 2][k % 2] = rows_dot(probs.astype(BF16), value_b).astype(BF16)


def backward_kernel(last, pairs, info_ref, *refs):
    token_ref, scale_ref, fold_ref = refs[:3]
    refs = refs[3:]
    blocks = member_blocks(refs[:pairs], refs[pairs])
    before_ref = refs[pairs + 1] if last else None
    out_ref, work, grads = refs[-3:]
    tokens, onehot = project(info_ref, token_ref, fold_ref, work)
    place_sum = jnp.zeros((TOK, KINDS * HD), F32)
    for k in range(token_ref.shape[0]):
        patch = jnp.bitwise_xor(info_ref[0], k)
        scale, query, key, value_b, probs = attend(patch, k, scale_ref, work)
        query_n, query_r, query_b = query
        key_n, key_r, key_b = key
        d_att = blocks[k][...]
        d_probs = last_dot(d_att, value_b)
        d_value = first_dot(probs.astype(BF16), d_att)
        row_total = jnp.sum(d_probs * probs, axis=-1, keepdims=True)
        d_logits = (probs * (d_probs - row_total) * (1.0 / HD**0.5)).astype(BF16)
        d_query_n = rows_dot(d_logits, key_b)
        d_key_n = first_dot(d_logits, query_b)
        d_query = query_r * (
            d_query_n - query_n * jnp.mean(d_query_n * query_n, axis=-1, keepdims=True)
        )
        d_key = key_r * (d_key_n - key_n * jnp.mean(d_key_n * key_n, axis=-1, keepdims=True))
        grad = jnp.concatenate([d_query * scale, d_key * scale, d_value * scale], axis=1)
        place_sum += grad
        grads[pl.ds(pl.multiple_of(patch * TOK, TOK), TOK), :] = grad.astype(BF16)
    all_grads = grads[...]
    parts = (first_dot(tokens, all_grads), place_sum, first_dot(onehot, all_grads))
    start = 0
    for part in parts:
        rows = part.shape[0]
        for kind in range(KINDS):
            block = part[:, kind * HD : (kind + 1) * HD]
            if last:
                block += before_ref[kind, start : start + rows]
            out_ref[kind, start : start + rows] = block.astype(out_ref.dtype)
        start += rows


def forward_heads(info, tokens, scale, folds):
    heads = scale.shape[0]
    return pl.pallas_call(
        forward_kernel,
        in_specs=[pl.BlockSpec(memory_space=SMEM)] + [pl.BlockSpec(memory_space=VMEM)] * 3,
        out_specs=[pl.BlockSpec(memory_space=VMEM)] * (heads // 2),
        out_shape=[jax.ShapeDtypeStruct((2, TOK, HD), BF16)] * (heads // 2),
        scratch_shapes=[pltpu.VMEM((heads, TOK, KINDS * HD), F32)],
        compiler_params=PARAMS,
        cost_estimate=cost(5),
        name="forward_heads",
    )(info, tokens, scale, folds)


def backward_heads(info, tokens, scale, folds, pairs, other, before):
    heads = scale.shape[0]
    last = before is not None
    operands = [*pairs, other] + ([before] if last else [])
    return pl.pallas_call(
        functools.partial(backward_kernel, last, len(pairs)),
        in_specs=[pl.BlockSpec(memory_space=SMEM)]
        + [pl.BlockSpec(memory_space=VMEM)] * (3 + len(operands)),
        out_specs=pl.BlockSpec(memory_space=VMEM),
        out_shape=jax.ShapeDtypeStruct((KINDS,) + folds.shape[1:], BF16 if last else F32),
        scratch_shapes=[
            pltpu.VMEM((heads, TOK, KINDS * HD), F32),
            pltpu.VMEM((heads * TOK, KINDS * HD), BF16),
        ],
        compiler_params=pltpu.CompilerParams(vmem_limit_bytes=28 * 1024 * 1024),
        cost_estimate=cost(9),
        name="backward_heads",
    )(info, tokens, scale, folds, *operands)


def output_kernel(number, pairs, me_ref, *refs):
    operands, outs = refs[:4], refs[pairs + 5 : 2 * pairs + 9]
    work, buffers, sems = refs[-6], refs[-5:-1], refs[-1]
    sources = [operands[0].at[number], operands[1], operands[2].at[number], operands[3]]
    copies = start_loads(sources, buffers, sems)
    cot_ref, unembed_ref, hidden_ref, w_ref = buffers
    blocks = member_blocks(refs[4 : 4 + pairs], refs[4 + pairs])
    score_ref, same_ref, other_ref, d_hidden_ref = outs[:4]
    d_att_refs = outs[4:]
    me = me_ref[0]
    finish(copies[:2])
    d_feat = last_dot(cot_ref[...], unembed_ref[...])
    finish(copies[2:])
    for k, block in enumerate(blocks):
        at = pl.multiple_of(jnp.bitwise_xor(me, k) * HD, HD)
        work[:, pl.ds(at, HD)] = block[...]
        at = pl.multiple_of(jnp.bitwise_xor(me, k) // 2 * HD, HD)
        (other_ref if k % 2 else same_ref)[:, pl.ds(at, HD)] = block[...]
    hidden = hidden_ref[...] + rows_dot(work[...], w_ref[...])
    centre = hidden - jnp.mean(hidden, axis=-1, keepdims=True)
    inverse = lax.rsqrt(jnp.mean(centre * centre, axis=-1, keepdims=True) + 1e-05)
    feat = centre * inverse
    score_ref[...] = rows_dot(feat.astype(BF16), unembed_ref[...])
    d_hidden = inverse * (
        d_feat
        - jnp.mean(d_feat, axis=-1, keepdims=True)
        - feat * jnp.mean(d_feat * feat, axis=-1, keepdims=True)
    )
    d_hidden = d_hidden.astype(BF16)
    d_hidden_ref[...] = d_hidden
    work[...] = last_dot(d_hidden, w_ref[...]).astype(BF16)
    for k in range(len(blocks)):
        at = pl.multiple_of(jnp.bitwise_xor(me, k) * HD, HD)
        d_att_refs[k // 2][k % 2] = work[:, pl.ds(at, HD)]


def output_part(number, me, hidden, cot, w_out, unembed, pairs, other):
    inner, width = w_out.shape
    operands = [cot, unembed, hidden, w_out]
    shapes = [cot[0], unembed, hidden[0], w_out]
    shape = jax.ShapeDtypeStruct
    return pl.pallas_call(
        functools.partial(output_kernel, number, len(pairs)),
        in_specs=[pl.BlockSpec(memory_space=SMEM)]
        + [pl.BlockSpec(memory_space=HBM)] * 4
        + [pl.BlockSpec(memory_space=VMEM)] * (1 + len(pairs)),
        out_specs=[pl.BlockSpec(memory_space=VMEM)] * (4 + len(pairs)),
        out_shape=[
            shape((TOK, VOX), F32),
            shape((TOK, inner // 2), BF16),
            shape((TOK, inner // 2), BF16),
            shape((TOK, width), BF16),
        ]
        + [shape((2, TOK, HD), BF16)] * len(pairs),
        scratch_shapes=[pltpu.VMEM((TOK, inner), BF16)] + load_scratch(shapes),
        compiler_params=pltpu.CompilerParams(vmem_limit_bytes=56 * 1024 * 1024),
        cost_estimate=cost(8),
        name="output_part",
    )(me, *operands, *pairs, other)


def expand_kernel(heads, number, me_ref, embed_ref, pos_ref, level_ref, *refs):
    out_refs, work = refs[number:-1], refs[-1]
    total = refs[0][...].astype(F32)
    for ref in refs[1:number]:
        total += ref[...].astype(F32)
    total = total.astype(BF16)
    split = embed_ref.shape[0]
    after = split + pos_ref.shape[0]
    grad = first_dot(embed_ref[...], total[:split])
    grad += first_dot(pos_ref[...], total[split:after])
    grad += first_dot(level_ref[...], total[after:])
    grad -= jnp.mean(grad, axis=0, keepdims=True)
    work[...] = grad.astype(BF16)
    depth = out_refs[0].shape[1]
    base = (me_ref[0] // heads) * heads
    for k in range(heads):
        member = base + jnp.bitwise_xor(lax.rem(me_ref[0], heads), k)
        at = pl.multiple_of(member * depth, depth)
        out_refs[k // 2][k % 2] = work[pl.ds(at, depth), :]


def expand_sums(me, heads, depth, embed, pos, level, own, others):
    width = embed.shape[1]
    columns = own.shape[1]
    return pl.pallas_call(
        functools.partial(expand_kernel, heads, 1 + len(others)),
        in_specs=[pl.BlockSpec(memory_space=SMEM)]
        + [pl.BlockSpec(memory_space=VMEM)] * 3
        + [pl.BlockSpec(memory_space=VMEM)] * (1 + len(others)),
        out_specs=[pl.BlockSpec(memory_space=VMEM)] * (heads // 2),
        out_shape=[jax.ShapeDtypeStruct((2, depth, columns), BF16)] * (heads // 2),
        scratch_shapes=[pltpu.VMEM((width, columns), BF16)],
        compiler_params=PARAMS,
        cost_estimate=cost(2),
        name="expand_sums",
    )(me, embed, pos, level, own, *others)


def columns_kernel(pairs, place_ref, *refs):
    blocks = member_blocks(refs[:pairs], refs[pairs])
    for k, block in enumerate(blocks):
        for kind, out_ref in enumerate(refs[pairs + 1 :]):
            index = jnp.bitwise_xor(place_ref[0], k) - place_ref[1 + kind]

            @pl.when((index >= 0) & (index < out_ref.shape[1] // HD))
            def _():
                at = pl.multiple_of(index * HD, HD)
                out_ref[:, pl.ds(at, HD)] = block[:, kind * HD : (kind + 1) * HD].astype(F32)


def join_columns(place, qk_heads, v_heads, pairs, other):
    depth = other.shape[1]
    return pl.pallas_call(
        functools.partial(columns_kernel, len(pairs)),
        in_specs=[pl.BlockSpec(memory_space=SMEM)]
        + [pl.BlockSpec(memory_space=VMEM)] * (1 + len(pairs)),
        out_specs=[pl.BlockSpec(memory_space=VMEM)] * 2,
        out_shape=[jax.ShapeDtypeStruct((depth, n * HD), F32) for n in (qk_heads, v_heads)],
        compiler_params=PARAMS,
        cost_estimate=cost(1),
        name="join_columns",
    )(place, *pairs, other)


def on_device(
    slabs,
    members,
    volume,
    noise,
    cotangent,
    patch_corner,
    patch_count,
    patch_level,
    embed,
    unembed,
    level_table,
    pos_embed,
    w_qkv,
    w_out,
):
    planes, side = volume.shape[:2]
    width = embed.shape[1]
    inner = w_out.shape[0] * members
    heads = inner // HD
    groups = members // heads
    depth = w_qkv.shape[0]
    slab = lax.axis_index("slab")
    member = lax.axis_index("fsdp")
    group, head = member // heads, member % heads

    def in_group(block, k):
        pairs = [(i, (i // heads) * heads + ((i % heads) ^ k)) for i in range(members)]
        return swap(block, "fsdp", pairs)

    def among_slabs(block, k):
        return across(block, "slab", slabs, k)

    def to_chips(pairs, move):
        return [move(pair, 2 * i) if i else pair for i, pair in enumerate(pairs)]

    def for_cores(landed):
        return pack_seconds(list(landed))

    me = jnp.reshape(member, (1,)).astype(jnp.int32)
    core = member % 2

    part = HALO // 2

    def rims_to_send(*fields):
        return jnp.stack(
            [lax.dynamic_slice(f, (core * part, 0, 0), (part, side, side)) for f in fields]
        )

    def rims_of(rims, *others):
        rims = after(swap(rims, "slab", [(i, i - 1) for i in range(1, slabs)]), *others)
        return rims, across(rims, "fsdp", members, 1)

    rims_sent = rims_to_send(volume, noise)

    total = members * PPD
    all_corner, all_level = pick_patches(
        patch_count[0], patch_corner[0], patch_level[0], 0, total
    )
    group_first = group * heads * PPD
    corner = lax.dynamic_slice(all_corner, (group_first, 0), (heads * PPD, 3))
    level = lax.dynamic_slice(all_level, (group_first,), (heads * PPD,))
    corner = jnp.stack([corner[:, 0] - slab * planes, corner[:, 1] // 8, corner[:, 2]], axis=1)
    own_corner = lax.dynamic_slice(corner, (head * PPD, 0), (PPD, 3))
    levels = jnp.stack([among_slabs(all_level, k) if k else all_level for k in range(slabs)])
    w_qkv = after(w_qkv, levels)
    levels = jnp.take(levels, jnp.arange(slabs, dtype=jnp.int32) ^ slab, axis=0).reshape(-1)

    kind = slab % KINDS
    w_pairs = []
    for k in range(0, members, 2):
        pair = [
            lax.dynamic_slice(
                w_qkv, (0, kind * inner + ((member ^ (k + j)) % heads) * HD), (depth, HD)
            )
            for j in range(2)
        ]
        w_pairs.append(jnp.stack(pair))
    w_pairs = to_chips(w_pairs, lambda x, k: across(x, "fsdp", members, k))

    onehot = (levels[:, None] == jnp.arange(level_table.shape[0], dtype=jnp.int32)[None, :]).astype(
        BF16
    )
    level_rows = jnp.dot(onehot, level_table, preferred_element_type=F32).astype(BF16)

    pos = pos_embed.reshape(PZT * PXY, PXY, width).transpose(1, 0, 2).reshape(TOK, width)

    factors = jnp.stack(noise_factors(level), axis=1)
    own_factors = lax.dynamic_slice(factors, (head * PPD, 0), (PPD, 2))
    core_of = jnp.reshape(core, (1,)).astype(jnp.int32)
    order = lane_order()
    rims, other_rims = rims_of(rims_sent, order, pos, level_rows)
    own_tokens, clean, noisy = join_and_cut(
        core_of, own_corner, own_factors, order, (volume, noise), rims, other_rims
    )
    own_place = slab * total + member * PPD
    own_rows = lax.dynamic_slice(level_rows, (own_place, 0), (PPD, width)).astype(F32)
    hidden = jnp.dot(own_tokens.reshape(PPD * TOK, VOX), embed, preferred_element_type=F32)
    hidden = hidden.reshape(PPD, TOK, width) + own_rows[:, None, :] + pos.astype(F32)[None]
    centre = hidden - jnp.mean(hidden, axis=-1, keepdims=True)
    scale = lax.rsqrt(jnp.mean(centre * centre, axis=-1) + 1e-05)[None]
    scale = scale.astype(F32)
    w_out = after(w_out, w_pairs)
    w_other = across(for_cores(w_pairs), "fsdp", members, 1)
    fold = fold_weights(me, embed, pos, level_rows, *after((w_pairs, w_other), scale))
    fold_pieces = [among_slabs(fold, k) if k else fold for k in range(slabs)]
    tokens = []
    step = 1
    for n in range(PPD):
        clean, noisy = after((clean, noisy), fold, scale, tokens)
        tokens.append(cut_tokens(corner[n::PPD], factors[n::PPD], order, clean, noisy))
        if step < heads:
            scale = jnp.concatenate([scale, in_group(scale, step)], axis=0)
            step *= 2
    folds = jnp.stack(after(fold_pieces, tokens))
    while step < heads:
        scale = jnp.concatenate([scale, in_group(scale, step)], axis=0)
        step *= 2
    scales = [scale[:, n].reshape(heads, 1, TOK) for n in range(PPD)]

    tangents, _ = join_and_cut(
        core_of,
        own_corner,
        own_factors,
        order,
        (cotangent,),
        *rims_of(rims_to_send(after(cotangent, tokens))),
    )
    full_out = lax.all_gather(w_out, "fsdp", axis=0, tiled=True)

    infos = [
        jnp.stack([head, slab * total + group_first + n] + [slab ^ j for j in range(KINDS)]).astype(
            jnp.int32
        )
        for n in range(PPD)
    ]
    head_me = jnp.reshape(head, (1,)).astype(jnp.int32)
    def output_of(n, landed, other):
        score, same, diff, d_hidden, *d_att = output_part(
            n, head_me, hidden, tangents, full_out, unembed, landed, other
        )
        return (score, same, diff, d_hidden), d_att

    results, sends, returns = [], [], []
    att = forward_heads(infos[0], tokens[0], scales[0], folds)
    landed = to_chips(att, in_group)
    for n in range(PPD):
        crossing = for_cores(landed)
        if returns:
            returns = to_chips(after(returns, crossing), in_group)
            sends.append(returns)
        if n + 1 < PPD:
            att = forward_heads(infos[n + 1], tokens[n + 1], scales[n + 1], folds)
            coming = to_chips(after(att, crossing), in_group)
        result, returns = output_of(n, landed, in_group(crossing, 1))
        results.append(result)
        if n + 1 < PPD:
            landed = after(coming, returns)
    scores, sames, diffs, d_hiddens = zip(*results)
    crossing = for_cores(after(sends[0], returns))
    sends.append(to_chips(after(returns, crossing), in_group))
    sames, diffs, d_hiddens = after((sames, diffs, d_hiddens), crossing)

    d_hidden = jnp.concatenate(d_hiddens, axis=0)
    away = first_dot(jnp.concatenate(diffs, axis=0), d_hidden).astype(BF16)
    away_sent = away
    if groups == 1:
        away = across(away, "fsdp", members, 1)

    buffer = place_scores(own_corner, after(scores, away_sent), planes + HALO, side)
    pairs, other = after((sends[0], in_group(crossing, 1)), buffer)
    summed = lax.psum_scatter(buffer, "fsdp", scatter_dimension=1, tiled=True)
    sums = backward_heads(infos[0], tokens[0], scales[0], folds, pairs, other, None)
    crossing = for_cores(after(sends[1], sums))
    stay = first_dot(
        jnp.concatenate(sames, axis=0), after(d_hidden, crossing)
    )
    if groups > 1:
        both = [stay.astype(BF16).reshape(-1, HD, width), away.reshape(-1, HD, width)]
        even = jnp.where(core == 0, both[0], both[1])
        odd = jnp.where(core == 0, both[1], both[0])
        out_sum = jnp.stack([even, odd], axis=1).reshape(inner, width)
    else:
        out_sum = (stay + away.astype(F32)).astype(BF16)
    columns = width // slabs

    def for_slab(k):
        return lax.dynamic_slice(out_sum, (0, (slab ^ k) * columns), (out_sum.shape[0], columns))

    slab_parts = [among_slabs(for_slab(k), k) for k in range(1, slabs)]

    before, pairs, other = after((sums, sends[1], in_group(crossing, 1)), out_sum)
    sums = backward_heads(infos[1], tokens[1], scales[1], folds, pairs, other, before)

    half = slabs // 2

    def sums_for(target):
        qk = lax.dynamic_index_in_dim(sums, target // half, 0, keepdims=False)
        return jnp.concatenate([qk, sums[2]], axis=1)

    qk_heads = heads // half
    v_heads = heads // slabs

    def owns(s, h):
        return (h // qk_heads == s % half, h // v_heads == s)

    def to_owner(k):
        pairs = [
            (s * members + i, (s ^ k) * members + i)
            for s in range(slabs)
            for i in range(members)
            if any(owns(s ^ k, i % heads))
        ]
        return swap(sums_for(slab ^ k), ("slab", "fsdp"), pairs)

    others = [to_owner(k) for k in range(1, slabs)]
    own = sums_for(slab)
    if groups > 1:
        gathered = own.astype(F32)
        for block in others:
            gathered += block.astype(F32)
        own = gathered.astype(BF16)
        others = []
        for g in range(1, groups):
            route = [(i, ((i // heads) ^ g) * heads + i % heads) for i in range(members)]
            others.append(swap(own, "fsdp", route))
    blocks = expand_sums(me, heads, depth, embed, pos, level_rows, own, others)
    pairs_of = []
    for k in range(heads):
        pairs = []
        for s in range(slabs):
            for i in range(members):
                h = i % heads
                if any(owns(s, h)):
                    j = (i // heads) * heads + (h ^ k)
                    pairs.append((s * members + i, s * members + j))
        pairs_of.append(pairs)
    slab_sum = for_slab(0).astype(F32)
    for block in slab_parts:
        slab_sum += block.astype(F32)
    slab_sum = slab_sum.astype(BF16)
    if groups > 1:
        grad_out = lax.psum_scatter(slab_sum, "fsdp", scatter_dimension=0, tiled=True).astype(F32)
    else:

        def for_chip(k):
            return lax.dynamic_slice(slab_sum, ((member ^ k) // 2 * HD, 0), (HD, columns))

        chip_sends = after([for_chip(k) for k in range(2, members, 2)], blocks)
        grad_out = for_chip(0).astype(F32)
        for i, send in enumerate(chip_sends):
            grad_out += across(send, "fsdp", members, 2 * i + 2).astype(F32)

    arrived = to_chips(blocks, lambda x, k: swap(x, ("slab", "fsdp"), pairs_of[k]))
    rim = summed[planes:]
    arrived = after(arrived, rim)
    arrived_other = in_group(for_cores(arrived), 1)
    place = jnp.stack([head, (slab % half) * qk_heads, slab * v_heads]).astype(jnp.int32)
    grad_qk, grad_v = join_columns(place, qk_heads, v_heads, arrived, arrived_other)

    arrived_rim = swap(rim, "slab", [(i, i + 1) for i in range(slabs - 1)])
    score = summed[:planes].astype(F32).at[:HALO].add(arrived_rim.astype(F32))
    return (score, grad_qk, grad_v, grad_out)


def solution(mesh):
    placed = (
        P("slab", None, None),
        P("slab", None, None),
        P("slab", None, None),
        P("slab", None, None),
        P("slab", None),
        P("slab", None),
        P(),
        P(),
        P(),
        P(),
        P("fsdp", None),
        P("fsdp", None),
    )
    return jax.shard_map(
        functools.partial(on_device, mesh.shape["slab"], mesh.shape["fsdp"]),
        mesh=mesh,
        in_specs=placed,
        out_specs=(
            P("slab", "fsdp", None),
            P("fsdp", "slab"),
            P("fsdp", "slab"),
            P("fsdp", "slab"),
        ),
        check_vma=False,
    )
```

```python
import functools

import jax
import jax.numpy as jnp
from jax import lax
from jax.experimental import pallas as pl
from jax.experimental.pallas import tpu as pltpu
from jax.sharding import PartitionSpec as P

HD = 128
NLEV = 1000
EDGE = 8
PXY = 8
PZT = 4
PPD = 2
HALO = 24
TOK = PZT * PXY * PXY
VOX = EDGE * EDGE * EDGE
KINDS = 3
LANES = 128

F32 = jnp.float32
BF16 = jnp.bfloat16
VMEM = pltpu.MemorySpace.VMEM
SMEM = pltpu.MemorySpace.SMEM
HBM = pltpu.MemorySpace.HBM
PARAMS = pltpu.CompilerParams(vmem_limit_bytes=20 * 1024 * 1024)


def cost(microseconds):
    return pl.CostEstimate(
        flops=int(microseconds * 1e9), bytes_accessed=1 << 20, transcendentals=0
    )


def swap(block, axis, pairs):
    return lax.ppermute(block, axis, pairs)


def after(value, *others):
    return lax.optimization_barrier((value, others))[0]


def across(block, axis, size, k):
    return lax.ppermute(block, axis, [(i, i ^ k) for i in range(size)])


def rows_dot(left, right):
    return lax.dot_general(left, right, (((1,), (0,)), ((), ())), preferred_element_type=F32)


def last_dot(left, right):
    return lax.dot_general(left, right, (((1,), (1,)), ((), ())), preferred_element_type=F32)


def first_dot(left, right):
    return lax.dot_general(left, right, (((0,), (0,)), ((), ())), preferred_element_type=F32)


def pick_patches(counts, corners, levels, first, number):
    slots = corners.shape[0] // counts.shape[0]
    live = (
        (jnp.arange(slots, dtype=jnp.int32)[None, :] < counts[:, None])
        .reshape(-1)
        .astype(jnp.int32)
    )
    before = jnp.cumsum(live, dtype=jnp.int32) - live
    wanted = first + jnp.arange(number, dtype=jnp.int32)
    chosen = ((before[None, :] == wanted[:, None]) & (live[None, :] == 1)).astype(jnp.int32)
    chosen_corner = jnp.sum(chosen[:, :, None] * corners[None, :, :], axis=1, dtype=jnp.int32)
    chosen_level = jnp.sum(chosen * levels[None, :], axis=1, dtype=jnp.int32)
    return (chosen_corner, chosen_level)


def noise_factors(chosen_level):
    sigma_level = 0.5 * jnp.exp(jnp.log(8.0) * chosen_level.astype(F32) / (NLEV - 1))
    return (sigma_level, lax.rsqrt(1.0 + sigma_level * sigma_level))


def exchange_groups(tiles, lane):
    for bit in range(3):
        step = 1 << bit
        upper = ((lane >> (3 + bit)) & 1) == 1
        fresh = []
        for i in range(8):
            other = tiles[i ^ step]
            if i & step:
                moved = pltpu.roll(other, LANES - 8 * step, 1)
                fresh.append(jnp.where(upper, tiles[i], moved))
            else:
                moved = pltpu.roll(other, 8 * step, 1)
                fresh.append(jnp.where(upper, moved, tiles[i]))
        tiles = fresh
    return tiles


def lane_order():
    row = lax.broadcasted_iota(jnp.int32, (8 * LANES, 8 * LANES), 0)
    lane = lax.broadcasted_iota(jnp.int32, (8 * LANES, 8 * LANES), 1)
    source = (lane // 8) % 8 * LANES + (lane // 64) % 2 * 64 + lane // LANES * 8 + lane % 8
    return (row == source).astype(BF16)


def cut_patches(count, corner_ref, factor_ref, order_ref, fields, pairs, work, wide, out_ref):
    row = lax.broadcasted_iota(jnp.int32, (2 * LANES, LANES), 0)
    lane = lax.broadcasted_iota(jnp.int32, (2 * LANES, LANES), 1)
    source = lane // 64 * LANES + lane % 64

    def body(number, carry):
        z0 = corner_ref[number, 0]
        y0 = corner_ref[number, 1]
        for pz in range(PZT):
            for ez in range(EDGE):
                z = z0 + pz * EDGE + ez
                plane = fields[0][z, pl.ds(y0, PXY)].astype(F32)
                if len(fields) == 2:
                    noise = fields[1][z, pl.ds(y0, PXY)].astype(F32)
                    plane = (plane + factor_ref[number, 0] * noise) * factor_ref[number, 1]
                at = (pz * 4 + ez // 2) * 64
                half = ez % 2 * LANES
                pairs[at : at + 64, half : half + LANES] = plane.reshape(64, LANES).astype(BF16)
        select = (row == source + corner_ref[number, 2]).astype(BF16)
        work[...] = rows_dot(pairs[...], select)
        at = pl.multiple_of(number * LANES, LANES)
        for ey in range(EDGE):
            tile = work[pl.ds(ey, LANES, stride=8), :]
            wide[pl.ds(at, LANES), ey * LANES : (ey + 1) * LANES] = tile.astype(BF16)
        return carry

    lax.fori_loop(0, count, body, 0)
    for two in range(PXY // 2):
        moved = rows_dot(wide[...], order_ref[:, two * 2 * LANES : (two + 1) * 2 * LANES])
        for number in range(count):
            for pair in range(PZT // 2):
                for ez in range(EDGE // 2):
                    first = number * LANES + (2 * pair * 4 + ez) * 8
                    second = first + 4 * 8
                    both = jnp.concatenate(
                        [moved[first : first + 8], moved[second : second + 8]], axis=0
                    ).astype(BF16)
                    for px in range(2):
                        at = (two * 2 + px) * 32 + pair * 16
                        out_ref[number, at : at + 16, ez * LANES : (ez + 1) * LANES] = both[
                            :, px * LANES : (px + 1) * LANES
                        ]


def cut_scratch(count):
    return [
        pltpu.VMEM((16 * 64, 2 * LANES), BF16),
        pltpu.VMEM((16 * 64, LANES), F32),
        pltpu.VMEM((count * LANES, 8 * LANES), BF16),
    ]


def join_kernel(count, number, core_ref, corner_ref, factor_ref, order_ref, *refs):
    field_refs, (mine_ref, other_ref) = refs[:number], refs[number : number + 2]
    out_ref, joined, scratch = refs[number + 2], refs[number + 3 : -3], refs[-3:]
    planes = field_refs[0].shape[0]
    part = mine_ref.shape[1]
    core = core_ref[0]
    for i in range(number):
        joined[i][:planes] = field_refs[i][...]
        joined[i][pl.ds(planes + part * core, part)] = mine_ref[i]
        joined[i][pl.ds(planes + part * (1 - core), part)] = other_ref[i]
    cut_patches(count, corner_ref, factor_ref, order_ref, joined, *scratch, out_ref)


def in_cells(field):
    return field.reshape(field.shape[:-2] + (field.shape[-2] // 8, 8, LANES))


def join_and_cut(core, corner, factors, order, fields, mine, other):
    count = corner.shape[0]
    number = len(fields)
    fields = [in_cells(f) for f in fields]
    mine, other = in_cells(mine), in_cells(other)
    joined = (fields[0].shape[0] + 2 * mine.shape[1],) + fields[0].shape[1:]
    return pl.pallas_call(
        functools.partial(join_kernel, count, number),
        in_specs=[pl.BlockSpec(memory_space=SMEM)] * 3
        + [pl.BlockSpec(memory_space=VMEM)] * (number + 3),
        out_specs=[pl.BlockSpec(memory_space=VMEM)] * (number + 1),
        out_shape=[jax.ShapeDtypeStruct((count, TOK, VOX), BF16)]
        + [jax.ShapeDtypeStruct(joined, BF16)] * number,
        scratch_shapes=cut_scratch(count),
        compiler_params=PARAMS,
        cost_estimate=cost(4),
        name="join_and_cut",
    )(core, corner, factors, order, *fields, mine, other)


def cut_kernel(count, corner_ref, factor_ref, order_ref, *refs):
    fields, out_ref, scratch = refs[:2], refs[2], refs[3:]
    cut_patches(count, corner_ref, factor_ref, order_ref, fields, *scratch, out_ref)


def cut_tokens(corner, factors, order, clean, noisy):
    count = corner.shape[0]
    return pl.pallas_call(
        functools.partial(cut_kernel, count),
        in_specs=[pl.BlockSpec(memory_space=SMEM)] * 2 + [pl.BlockSpec(memory_space=VMEM)] * 3,
        out_specs=pl.BlockSpec(memory_space=VMEM),
        out_shape=jax.ShapeDtypeStruct((count, TOK, VOX), BF16),
        scratch_shapes=cut_scratch(count),
        compiler_params=PARAMS,
        cost_estimate=cost(7),
        name="cut_tokens",
    )(corner, factors, order, clean, noisy)


def place_kernel(corner_ref, *refs):
    score_refs = refs[:PPD]
    out_ref, buffer, work = refs[PPD:]
    lane = lax.broadcasted_iota(jnp.int32, (8, LANES), 1)
    wide = lax.broadcasted_iota(jnp.int32, (64, LANES), 1)
    buffer[...] = jnp.zeros_like(buffer)
    for number in range(PPD):
        z0 = corner_ref[number, 0]
        y0 = corner_ref[number, 1]
        x0 = corner_ref[number, 2]
        inside = (wide >= x0) & (wide < x0 + 64)
        for pz in range(PZT):
            for ez in range(0, EDGE, 2):
                tiles = [
                    score_refs[number][
                        px * 32 + pz * 8 : px * 32 + pz * 8 + 8,
                        (ez // 2) * LANES : (ez // 2 + 1) * LANES,
                    ].astype(F32)
                    for px in range(PXY)
                ]
                tiles = exchange_groups(tiles, lane)
                slot = pz * 4 + ez // 2
                for ey in range(8):
                    work[slot, pl.ds(ey, 8, stride=8), :] = tiles[ey]
                both = work[slot]
                for odd in range(2):
                    plane = pltpu.roll(both, lax.rem(LANES + x0 - 64 * odd, LANES), 1)
                    plane = jnp.where(inside, plane, 0.0).reshape(PXY, 8, LANES)
                    z = z0 + pz * EDGE + ez + odd
                    buffer[z, pl.ds(y0, PXY)] += plane
    out_ref[...] = buffer[...].astype(BF16)


def place_scores(corner, scores, planes, rows):
    shape = (planes, rows // 8, 8, LANES)
    out = pl.pallas_call(
        place_kernel,
        in_specs=[pl.BlockSpec(memory_space=SMEM)] + [pl.BlockSpec(memory_space=VMEM)] * PPD,
        out_specs=pl.BlockSpec(memory_space=VMEM),
        out_shape=jax.ShapeDtypeStruct(shape, BF16),
        scratch_shapes=[pltpu.VMEM(shape, F32), pltpu.VMEM((16, 64, LANES), F32)],
        compiler_params=PARAMS,
        cost_estimate=cost(6),
        name="place_scores",
    )(corner, *scores)
    return out.reshape(planes, rows, LANES)


def start_loads(refs, buffers, sems):
    copies = [
        pltpu.make_async_copy(ref, buffer, sems.at[i])
        for i, (ref, buffer) in enumerate(zip(refs, buffers))
    ]
    for copy in copies:
        copy.start()
    return copies


def finish(copies):
    for copy in copies:
        copy.wait()


def load_scratch(operands):
    return [pltpu.VMEM(x.shape, x.dtype) for x in operands] + [
        pltpu.SemaphoreType.DMA((len(operands),))
    ]


def member_blocks(pair_refs, other_ref):
    blocks = []
    for i, ref in enumerate(pair_refs):
        blocks += [ref.at[0], other_ref.at[i]]
    return blocks


def pack_kernel(*refs):
    for i, ref in enumerate(refs[:-1]):
        refs[-1][i] = ref[1]


def pack_seconds(pairs):
    return pl.pallas_call(
        pack_kernel,
        in_specs=[pl.BlockSpec(memory_space=VMEM)] * len(pairs),
        out_specs=pl.BlockSpec(memory_space=VMEM),
        out_shape=jax.ShapeDtypeStruct((len(pairs),) + pairs[0].shape[1:], pairs[0].dtype),
        cost_estimate=cost(1),
        name="pack_seconds",
    )(*pairs)


def fold_kernel(pairs, me_ref, embed_ref, pos_ref, level_ref, *refs):
    blocks, out_ref = member_blocks(refs[:pairs], refs[pairs]), refs[pairs + 1]
    me = me_ref[0]
    width = embed_ref.shape[1]
    depth = width // len(blocks)
    start = 0
    column = jnp.zeros((1, HD), F32)
    for block in blocks:
        column += jnp.sum(block[...].astype(F32), axis=0, keepdims=True)
    for part in (embed_ref, pos_ref, level_ref):
        rows = part.shape[0]
        total = jnp.zeros((rows, HD), F32)
        for k, block in enumerate(blocks):
            at = pl.multiple_of(jnp.bitwise_xor(me, k) * depth, LANES)
            total += rows_dot(part[:, pl.ds(at, depth)], block[...])
        mean = jnp.sum(part[...].astype(F32), axis=1, keepdims=True) / width
        out_ref[start : start + rows, :] = (total - mean * column).astype(BF16)
        start += rows


def fold_weights(me, embed, pos, level, pairs, other):
    rows = embed.shape[0] + pos.shape[0] + level.shape[0]
    return pl.pallas_call(
        functools.partial(fold_kernel, len(pairs)),
        in_specs=[pl.BlockSpec(memory_space=SMEM)]
        + [pl.BlockSpec(memory_space=VMEM)] * 3
        + [pl.BlockSpec(memory_space=VMEM)] * (1 + len(pairs)),
        out_specs=pl.BlockSpec(memory_space=VMEM),
        out_shape=jax.ShapeDtypeStruct((rows, HD), BF16),
        compiler_params=PARAMS,
        cost_estimate=cost(2),
        name="fold_weights",
    )(me, embed, pos, level, *pairs, other)


def head_normal(values):
    inverse = lax.rsqrt(jnp.mean(values * values, axis=-1, keepdims=True) + 1e-06)
    return (values * inverse, inverse)


def project(info_ref, token_ref, fold_ref, work):
    count = token_ref.shape[0]
    patches = fold_ref.shape[1] - VOX - TOK
    tokens = token_ref[...].reshape(count * TOK, VOX)
    row = lax.broadcasted_iota(jnp.int32, (count * TOK, patches), 0) // TOK
    place = info_ref[1] + row * PPD
    onehot = (lax.broadcasted_iota(jnp.int32, (count * TOK, patches), 1) == place).astype(BF16)
    for kind in range(KINDS):
        fold = fold_ref.at[info_ref[2 + kind]]
        total = rows_dot(tokens, fold[:VOX]) + rows_dot(onehot, fold[VOX + TOK :])
        pos = fold[VOX : VOX + TOK].astype(F32)
        for i in range(count):
            work[i, :, kind * HD : (kind + 1) * HD] = total[i * TOK : (i + 1) * TOK] + pos
    return tokens, onehot


def attend(patch, k, scale_ref, work):
    scale = jnp.transpose(jnp.broadcast_to(scale_ref[k], (HD, TOK)))
    kinds = [work[patch, :, j * HD : (j + 1) * HD] * scale for j in range(KINDS)]
    query_n, query_r = head_normal(kinds[0])
    key_n, key_r = head_normal(kinds[1])
    query_b, key_b, value_b = (query_n.astype(BF16), key_n.astype(BF16), kinds[2].astype(BF16))
    expo = jnp.exp(last_dot(query_b, key_b) * (1.0 / HD**0.5))
    probs = expo / jnp.sum(expo, axis=-1, keepdims=True)
    return (scale, (query_n, query_r, query_b), (key_n, key_r, key_b), value_b, probs)


def forward_kernel(info_ref, token_ref, scale_ref, fold_ref, *refs):
    out_refs, work = refs[:-1], refs[-1]
    project(info_ref, token_ref, fold_ref, work)
    for k in range(token_ref.shape[0]):
        patch = jnp.bitwise_xor(info_ref[0], k)
        _, _, _, value_b, probs = attend(patch, k, scale_ref, work)
        out_refs[k // 2][k % 2] = rows_dot(probs.astype(BF16), value_b).astype(BF16)


def backward_kernel(last, pairs, info_ref, *refs):
    token_ref, scale_ref, fold_ref = refs[:3]
    refs = refs[3:]
    blocks = member_blocks(refs[:pairs], refs[pairs])
    before_ref = refs[pairs + 1] if last else None
    out_ref, work, grads = refs[-3:]
    tokens, onehot = project(info_ref, token_ref, fold_ref, work)
    place_sum = jnp.zeros((TOK, KINDS * HD), F32)
    for k in range(token_ref.shape[0]):
        patch = jnp.bitwise_xor(info_ref[0], k)
        scale, query, key, value_b, probs = attend(patch, k, scale_ref, work)
        query_n, query_r, query_b = query
        key_n, key_r, key_b = key
        d_att = blocks[k][...]
        d_probs = last_dot(d_att, value_b)
        d_value = first_dot(probs.astype(BF16), d_att)
        row_total = jnp.sum(d_probs * probs, axis=-1, keepdims=True)
        d_logits = (probs * (d_probs - row_total) * (1.0 / HD**0.5)).astype(BF16)
        d_query_n = rows_dot(d_logits, key_b)
        d_key_n = first_dot(d_logits, query_b)
        d_query = query_r * (
            d_query_n - query_n * jnp.mean(d_query_n * query_n, axis=-1, keepdims=True)
        )
        d_key = key_r * (d_key_n - key_n * jnp.mean(d_key_n * key_n, axis=-1, keepdims=True))
        grad = jnp.concatenate([d_query * scale, d_key * scale, d_value * scale], axis=1)
        place_sum += grad
        grads[pl.ds(pl.multiple_of(patch * TOK, TOK), TOK), :] = grad.astype(BF16)
    all_grads = grads[...]
    parts = (first_dot(tokens, all_grads), place_sum, first_dot(onehot, all_grads))
    start = 0
    for part in parts:
        rows = part.shape[0]
        for kind in range(KINDS):
            block = part[:, kind * HD : (kind + 1) * HD]
            if last:
                block += before_ref[kind, start : start + rows]
            out_ref[kind, start : start + rows] = block.astype(out_ref.dtype)
        start += rows


def forward_heads(info, tokens, scale, folds):
    heads = scale.shape[0]
    return pl.pallas_call(
        forward_kernel,
        in_specs=[pl.BlockSpec(memory_space=SMEM)] + [pl.BlockSpec(memory_space=VMEM)] * 3,
        out_specs=[pl.BlockSpec(memory_space=VMEM)] * (heads // 2),
        out_shape=[jax.ShapeDtypeStruct((2, TOK, HD), BF16)] * (heads // 2),
        scratch_shapes=[pltpu.VMEM((heads, TOK, KINDS * HD), F32)],
        compiler_params=PARAMS,
        cost_estimate=cost(5),
        name="forward_heads",
    )(info, tokens, scale, folds)


def backward_heads(info, tokens, scale, folds, pairs, other, before):
    heads = scale.shape[0]
    last = before is not None
    operands = [*pairs, other] + ([before] if last else [])
    return pl.pallas_call(
        functools.partial(backward_kernel, last, len(pairs)),
        in_specs=[pl.BlockSpec(memory_space=SMEM)]
        + [pl.BlockSpec(memory_space=VMEM)] * (3 + len(operands)),
        out_specs=pl.BlockSpec(memory_space=VMEM),
        out_shape=jax.ShapeDtypeStruct((KINDS,) + folds.shape[1:], BF16 if last else F32),
        scratch_shapes=[
            pltpu.VMEM((heads, TOK, KINDS * HD), F32),
            pltpu.VMEM((heads * TOK, KINDS * HD), BF16),
        ],
        compiler_params=pltpu.CompilerParams(vmem_limit_bytes=28 * 1024 * 1024),
        cost_estimate=cost(9),
        name="backward_heads",
    )(info, tokens, scale, folds, *operands)


def output_kernel(number, pairs, me_ref, *refs):
    operands, outs = refs[:4], refs[pairs + 5 : 2 * pairs + 9]
    work, buffers, sems = refs[-6], refs[-5:-1], refs[-1]
    sources = [operands[0].at[number], operands[1], operands[2].at[number], operands[3]]
    copies = start_loads(sources, buffers, sems)
    cot_ref, unembed_ref, hidden_ref, w_ref = buffers
    blocks = member_blocks(refs[4 : 4 + pairs], refs[4 + pairs])
    score_ref, same_ref, other_ref, d_hidden_ref = outs[:4]
    d_att_refs = outs[4:]
    me = me_ref[0]
    finish(copies[:2])
    d_feat = last_dot(cot_ref[...], unembed_ref[...])
    finish(copies[2:])
    for k, block in enumerate(blocks):
        at = pl.multiple_of(jnp.bitwise_xor(me, k) * HD, HD)
        work[:, pl.ds(at, HD)] = block[...]
        at = pl.multiple_of(jnp.bitwise_xor(me, k) // 2 * HD, HD)
        (other_ref if k % 2 else same_ref)[:, pl.ds(at, HD)] = block[...]
    hidden = hidden_ref[...] + rows_dot(work[...], w_ref[...])
    centre = hidden - jnp.mean(hidden, axis=-1, keepdims=True)
    inverse = lax.rsqrt(jnp.mean(centre * centre, axis=-1, keepdims=True) + 1e-05)
    feat = centre * inverse
    score_ref[...] = rows_dot(feat.astype(BF16), unembed_ref[...])
    d_hidden = inverse * (
        d_feat
        - jnp.mean(d_feat, axis=-1, keepdims=True)
        - feat * jnp.mean(d_feat * feat, axis=-1, keepdims=True)
    )
    d_hidden = d_hidden.astype(BF16)
    d_hidden_ref[...] = d_hidden
    work[...] = last_dot(d_hidden, w_ref[...]).astype(BF16)
    for k in range(len(blocks)):
        at = pl.multiple_of(jnp.bitwise_xor(me, k) * HD, HD)
        d_att_refs[k // 2][k % 2] = work[:, pl.ds(at, HD)]


def output_part(number, me, hidden, cot, w_out, unembed, pairs, other):
    inner, width = w_out.shape
    operands = [cot, unembed, hidden, w_out]
    shapes = [cot[0], unembed, hidden[0], w_out]
    shape = jax.ShapeDtypeStruct
    return pl.pallas_call(
        functools.partial(output_kernel, number, len(pairs)),
        in_specs=[pl.BlockSpec(memory_space=SMEM)]
        + [pl.BlockSpec(memory_space=HBM)] * 4
        + [pl.BlockSpec(memory_space=VMEM)] * (1 + len(pairs)),
        out_specs=[pl.BlockSpec(memory_space=VMEM)] * (4 + len(pairs)),
        out_shape=[
            shape((TOK, VOX), F32),
            shape((TOK, inner // 2), BF16),
            shape((TOK, inner // 2), BF16),
            shape((TOK, width), BF16),
        ]
        + [shape((2, TOK, HD), BF16)] * len(pairs),
        scratch_shapes=[pltpu.VMEM((TOK, inner), BF16)] + load_scratch(shapes),
        compiler_params=pltpu.CompilerParams(vmem_limit_bytes=56 * 1024 * 1024),
        cost_estimate=cost(8),
        name="output_part",
    )(me, *operands, *pairs, other)


def expand_kernel(heads, number, me_ref, embed_ref, pos_ref, level_ref, *refs):
    out_refs, work = refs[number:-1], refs[-1]
    total = refs[0][...].astype(F32)
    for ref in refs[1:number]:
        total += ref[...].astype(F32)
    total = total.astype(BF16)
    split = embed_ref.shape[0]
    after = split + pos_ref.shape[0]
    grad = first_dot(embed_ref[...], total[:split])
    grad += first_dot(pos_ref[...], total[split:after])
    grad += first_dot(level_ref[...], total[after:])
    grad -= jnp.mean(grad, axis=0, keepdims=True)
    work[...] = grad.astype(BF16)
    depth = out_refs[0].shape[1]
    base = (me_ref[0] // heads) * heads
    for k in range(heads):
        member = base + jnp.bitwise_xor(lax.rem(me_ref[0], heads), k)
        at = pl.multiple_of(member * depth, depth)
        out_refs[k // 2][k % 2] = work[pl.ds(at, depth), :]


def expand_sums(me, heads, depth, embed, pos, level, own, others):
    width = embed.shape[1]
    columns = own.shape[1]
    return pl.pallas_call(
        functools.partial(expand_kernel, heads, 1 + len(others)),
        in_specs=[pl.BlockSpec(memory_space=SMEM)]
        + [pl.BlockSpec(memory_space=VMEM)] * 3
        + [pl.BlockSpec(memory_space=VMEM)] * (1 + len(others)),
        out_specs=[pl.BlockSpec(memory_space=VMEM)] * (heads // 2),
        out_shape=[jax.ShapeDtypeStruct((2, depth, columns), BF16)] * (heads // 2),
        scratch_shapes=[pltpu.VMEM((width, columns), BF16)],
        compiler_params=PARAMS,
        cost_estimate=cost(2),
        name="expand_sums",
    )(me, embed, pos, level, own, *others)


def columns_kernel(pairs, place_ref, *refs):
    blocks = member_blocks(refs[:pairs], refs[pairs])
    for k, block in enumerate(blocks):
        for kind, out_ref in enumerate(refs[pairs + 1 :]):
            index = jnp.bitwise_xor(place_ref[0], k) - place_ref[1 + kind]

            @pl.when((index >= 0) & (index < out_ref.shape[1] // HD))
            def _():
                at = pl.multiple_of(index * HD, HD)
                out_ref[:, pl.ds(at, HD)] = block[:, kind * HD : (kind + 1) * HD].astype(F32)


def join_columns(place, qk_heads, v_heads, pairs, other):
    depth = other.shape[1]
    return pl.pallas_call(
        functools.partial(columns_kernel, len(pairs)),
        in_specs=[pl.BlockSpec(memory_space=SMEM)]
        + [pl.BlockSpec(memory_space=VMEM)] * (1 + len(pairs)),
        out_specs=[pl.BlockSpec(memory_space=VMEM)] * 2,
        out_shape=[jax.ShapeDtypeStruct((depth, n * HD), F32) for n in (qk_heads, v_heads)],
        compiler_params=PARAMS,
        cost_estimate=cost(1),
        name="join_columns",
    )(place, *pairs, other)


def on_device(
    slabs,
    members,
    volume,
    noise,
    cotangent,
    patch_corner,
    patch_count,
    patch_level,
    embed,
    unembed,
    level_table,
    pos_embed,
    w_qkv,
    w_out,
):
    planes, side = volume.shape[:2]
    width = embed.shape[1]
    inner = w_out.shape[0] * members
    heads = inner // HD
    groups = members // heads
    depth = w_qkv.shape[0]
    slab = lax.axis_index("slab")
    member = lax.axis_index("fsdp")
    group, head = member // heads, member % heads

    def in_group(block, k):
        pairs = [(i, (i // heads) * heads + ((i % heads) ^ k)) for i in range(members)]
        return swap(block, "fsdp", pairs)

    def among_slabs(block, k):
        return across(block, "slab", slabs, k)

    def to_chips(pairs, move):
        return [move(pair, 2 * i) if i else pair for i, pair in enumerate(pairs)]

    def for_cores(landed):
        return pack_seconds(list(landed))

    me = jnp.reshape(member, (1,)).astype(jnp.int32)
    core = member % 2

    part = HALO // 2

    def rims_to_send(*fields):
        return jnp.stack(
            [lax.dynamic_slice(f, (core * part, 0, 0), (part, side, side)) for f in fields]
        )

    def rims_of(rims, *others):
        rims = after(swap(rims, "slab", [(i, i - 1) for i in range(1, slabs)]), *others)
        return rims, across(rims, "fsdp", members, 1)

    rims_sent = rims_to_send(volume, noise)

    total = members * PPD
    all_corner, all_level = pick_patches(
        patch_count[0], patch_corner[0], patch_level[0], 0, total
    )
    group_first = group * heads * PPD
    corner = lax.dynamic_slice(all_corner, (group_first, 0), (heads * PPD, 3))
    level = lax.dynamic_slice(all_level, (group_first,), (heads * PPD,))
    corner = jnp.stack([corner[:, 0] - slab * planes, corner[:, 1] // 8, corner[:, 2]], axis=1)
    own_corner = lax.dynamic_slice(corner, (head * PPD, 0), (PPD, 3))
    levels = jnp.stack([among_slabs(all_level, k) if k else all_level for k in range(slabs)])
    w_qkv = after(w_qkv, levels)
    levels = jnp.take(levels, jnp.arange(slabs, dtype=jnp.int32) ^ slab, axis=0).reshape(-1)

    kind = slab % KINDS
    w_pairs = []
    for k in range(0, members, 2):
        pair = [
            lax.dynamic_slice(
                w_qkv, (0, kind * inner + ((member ^ (k + j)) % heads) * HD), (depth, HD)
            )
            for j in range(2)
        ]
        w_pairs.append(jnp.stack(pair))
    w_pairs = to_chips(w_pairs, lambda x, k: across(x, "fsdp", members, k))

    onehot = (levels[:, None] == jnp.arange(level_table.shape[0], dtype=jnp.int32)[None, :]).astype(
        BF16
    )
    level_rows = jnp.dot(onehot, level_table, preferred_element_type=F32).astype(BF16)

    pos = pos_embed.reshape(PZT * PXY, PXY, width).transpose(1, 0, 2).reshape(TOK, width)

    factors = jnp.stack(noise_factors(level), axis=1)
    own_factors = lax.dynamic_slice(factors, (head * PPD, 0), (PPD, 2))
    core_of = jnp.reshape(core, (1,)).astype(jnp.int32)
    order = lane_order()
    rims, other_rims = rims_of(rims_sent, order, pos, level_rows)
    own_tokens, clean, noisy = join_and_cut(
        core_of, own_corner, own_factors, order, (volume, noise), rims, other_rims
    )
    own_place = slab * total + member * PPD
    own_rows = lax.dynamic_slice(level_rows, (own_place, 0), (PPD, width)).astype(F32)
    hidden = jnp.dot(own_tokens.reshape(PPD * TOK, VOX), embed, preferred_element_type=F32)
    hidden = hidden.reshape(PPD, TOK, width) + own_rows[:, None, :] + pos.astype(F32)[None]
    centre = hidden - jnp.mean(hidden, axis=-1, keepdims=True)
    scale = lax.rsqrt(jnp.mean(centre * centre, axis=-1) + 1e-05)[None]
    scale = scale.astype(F32)
    w_out = after(w_out, w_pairs)
    w_other = across(for_cores(w_pairs), "fsdp", members, 1)
    fold = fold_weights(me, embed, pos, level_rows, *after((w_pairs, w_other), scale))
    fold_pieces = [among_slabs(fold, k) if k else fold for k in range(slabs)]
    tokens = []
    step = 1
    for n in range(PPD):
        clean, noisy = after((clean, noisy), fold, scale, tokens)
        tokens.append(cut_tokens(corner[n::PPD], factors[n::PPD], order, clean, noisy))
        if step < heads:
            scale = jnp.concatenate([scale, in_group(scale, step)], axis=0)
            step *= 2
    folds = jnp.stack(after(fold_pieces, tokens))
    while step < heads:
        scale = jnp.concatenate([scale, in_group(scale, step)], axis=0)
        step *= 2
    scales = [scale[:, n].reshape(heads, 1, TOK) for n in range(PPD)]

    tangents, _ = join_and_cut(
        core_of,
        own_corner,
        own_factors,
        order,
        (cotangent,),
        *rims_of(rims_to_send(after(cotangent, tokens))),
    )
    full_out = lax.all_gather(w_out, "fsdp", axis=0, tiled=True)

    infos = [
        jnp.stack([head, slab * total + group_first + n] + [slab ^ j for j in range(KINDS)]).astype(
            jnp.int32
        )
        for n in range(PPD)
    ]
    head_me = jnp.reshape(head, (1,)).astype(jnp.int32)
    def output_of(n, landed, other):
        score, same, diff, d_hidden, *d_att = output_part(
            n, head_me, hidden, tangents, full_out, unembed, landed, other
        )
        return (score, same, diff, d_hidden), d_att

    results, sends, returns = [], [], []
    att = forward_heads(infos[0], tokens[0], scales[0], folds)
    landed = to_chips(att, in_group)
    for n in range(PPD):
        crossing = for_cores(landed)
        if returns:
            returns = to_chips(after(returns, crossing), in_group)
            sends.append(returns)
        if n + 1 < PPD:
            att = forward_heads(infos[n + 1], tokens[n + 1], scales[n + 1], folds)
            coming = to_chips(after(att, crossing), in_group)
        result, returns = output_of(n, landed, in_group(crossing, 1))
        results.append(result)
        if n + 1 < PPD:
            landed = after(coming, returns)
    scores, sames, diffs, d_hiddens = zip(*results)
    crossing = for_cores(after(sends[0], returns))
    sends.append(to_chips(after(returns, crossing), in_group))
    sames, diffs, d_hiddens = after((sames, diffs, d_hiddens), crossing)

    d_hidden = jnp.concatenate(d_hiddens, axis=0)
    away = first_dot(jnp.concatenate(diffs, axis=0), d_hidden).astype(BF16)
    away_sent = away
    if groups == 1:
        away = across(away, "fsdp", members, 1)

    buffer = place_scores(own_corner, after(scores, away_sent), planes + HALO, side)
    pairs, other = after((sends[0], in_group(crossing, 1)), buffer)
    summed = lax.psum_scatter(buffer, "fsdp", scatter_dimension=1, tiled=True)
    sums = backward_heads(infos[0], tokens[0], scales[0], folds, pairs, other, None)
    crossing = for_cores(after(sends[1], sums))
    stay = first_dot(
        jnp.concatenate(sames, axis=0), after(d_hidden, crossing)
    )
    if groups > 1:
        both = [stay.astype(BF16).reshape(-1, HD, width), away.reshape(-1, HD, width)]
        even = jnp.where(core == 0, both[0], both[1])
        odd = jnp.where(core == 0, both[1], both[0])
        out_sum = jnp.stack([even, odd], axis=1).reshape(inner, width)
    else:
        out_sum = (stay + away.astype(F32)).astype(BF16)
    columns = width // slabs

    def for_slab(k):
        return lax.dynamic_slice(out_sum, (0, (slab ^ k) * columns), (out_sum.shape[0], columns))

    slab_parts = [among_slabs(for_slab(k), k) for k in range(1, slabs)]

    before, pairs, other = after((sums, sends[1], in_group(crossing, 1)), out_sum)
    sums = backward_heads(infos[1], tokens[1], scales[1], folds, pairs, other, before)

    half = slabs // 2

    def sums_for(target):
        qk = lax.dynamic_index_in_dim(sums, target // half, 0, keepdims=False)
        return jnp.concatenate([qk, sums[2]], axis=1)

    qk_heads = heads // half
    v_heads = heads // slabs

    def owns(s, h):
        return (h // qk_heads == s % half, h // v_heads == s)

    def to_owner(k):
        pairs = [
            (s * members + i, (s ^ k) * members + i)
            for s in range(slabs)
            for i in range(members)
            if any(owns(s ^ k, i % heads))
        ]
        return swap(sums_for(slab ^ k), ("slab", "fsdp"), pairs)

    others = [to_owner(k) for k in range(1, slabs)]
    own = sums_for(slab)
    if groups > 1:
        gathered = own.astype(F32)
        for block in others:
            gathered += block.astype(F32)
        own = gathered.astype(BF16)
        others = []
        for g in range(1, groups):
            route = [(i, ((i // heads) ^ g) * heads + i % heads) for i in range(members)]
            others.append(swap(own, "fsdp", route))
    blocks = expand_sums(me, heads, depth, embed, pos, level_rows, own, others)
    pairs_of = []
    for k in range(heads):
        pairs = []
        for s in range(slabs):
            for i in range(members):
                h = i % heads
                if any(owns(s, h)):
                    j = (i // heads) * heads + (h ^ k)
                    pairs.append((s * members + i, s * members + j))
        pairs_of.append(pairs)
    slab_sum = for_slab(0).astype(F32)
    for block in slab_parts:
        slab_sum += block.astype(F32)
    slab_sum = slab_sum.astype(BF16)
    if groups > 1:
        grad_out = lax.psum_scatter(slab_sum, "fsdp", scatter_dimension=0, tiled=True).astype(F32)
    else:

        def for_chip(k):
            return lax.dynamic_slice(slab_sum, ((member ^ k) // 2 * HD, 0), (HD, columns))

        chip_sends = after([for_chip(k) for k in range(2, members, 2)], blocks)
        grad_out = for_chip(0).astype(F32)
        for i, send in enumerate(chip_sends):
            grad_out += across(send, "fsdp", members, 2 * i + 2).astype(F32)

    arrived = to_chips(blocks, lambda x, k: swap(x, ("slab", "fsdp"), pairs_of[k]))
    arrived_rim = swap(summed[planes:], "slab", [(i, i + 1) for i in range(slabs - 1)])
    arrived = after(arrived, arrived_rim)
    arrived_other = in_group(for_cores(arrived), 1)
    place = jnp.stack([head, (slab % half) * qk_heads, slab * v_heads]).astype(jnp.int32)
    grad_qk, grad_v = join_columns(place, qk_heads, v_heads, arrived, arrived_other)

    score = summed[:planes].astype(F32).at[:HALO].add(arrived_rim.astype(F32))
    return (score, grad_qk, grad_v, grad_out)


def solution(mesh):
    placed = (
        P("slab", None, None),
        P("slab", None, None),
        P("slab", None, None),
        P("slab", None, None),
        P("slab", None),
        P("slab", None),
        P(),
        P(),
        P(),
        P(),
        P("fsdp", None),
        P("fsdp", None),
    )
    return jax.shard_map(
        functools.partial(on_device, mesh.shape["slab"], mesh.shape["fsdp"]),
        mesh=mesh,
        in_specs=placed,
        out_specs=(
            P("slab", "fsdp", None),
            P("fsdp", "slab"),
            P("fsdp", "slab"),
            P("fsdp", "slab"),
        ),
        check_vma=False,
    )
```
